512 devices in a mesh: rows: 32 (over x, z), vecs: 16 (over y, core).
Axes of the slice: x: 4, y: 8, z: 8, core: 2. Of those that a mesh axis runs over, the one named last changes fastest.
Arguments:
- tiles: bfloat16 [128, 6, 128, 128], P('rows'), as said below
- columns: int32 [128, 6], P('rows'), may hold values from 0 to 127, as said below
- start_vectors: float32 [1024, 16384], P('vecs', 'rows'), may hold values from -6 to 6
Outputs:
- basis: float32 [1024, 16384], P('vecs', 'rows')
The draws below stay inside these ranges and needn't reach their ends.
Inputs may be any that keep to these rules, and one draw needn't show every extreme that they name: `columns`: the 6 column blocks of row block b are distinct; they are b, b - 1, b + 1 and three of b - 3, b - 2, b + 2, b + 3, all modulo 128, the first three in this order. The pattern is symmetric: block c is among those of row block b exactly when b is among those of row block c. `tiles`: H is symmetric: the tile of row block b at column block c is the transpose of the tile of row block c at column block b.
All inputs are finite; a program needn't handle non-finite values.
Results may differ from the reference program's by a relative error of at most 0.0003.
Values sent between devices are 32-bit elements; how exact they have to be, the bound alone decides.
A program may use at most 64 MiB of HBM per device.

```python
import jax
import jax.numpy as jnp
from jax import lax

M = 1024
BS = 128
STEPS = 4
NBLK = 128
NROW = 16384


def block_offsets(key):
    pattern_key = jax.random.fold_in(key, 7)
    phase_key, order_key = jax.random.split(pattern_key)
    phase = jax.random.randint(phase_key, (), 0, 4, dtype=jnp.int32)
    base = jnp.arange(NBLK, dtype=jnp.int32)
    position = jnp.mod(base - phase, 4)
    missing = jnp.where(position < 2, 2, -2).astype(jnp.int32)
    farther = jnp.array([-3, -2, 2, 3], dtype=jnp.int32)
    keep = farther[None, :] != missing[:, None]
    ranks = jnp.where(keep, jnp.arange(4, dtype=jnp.int32)[None, :], 4)
    chosen = jnp.argsort(ranks, axis=1, stable=True)[:, :3]
    kept = farther[chosen]
    row_keys = jax.random.split(order_key, NBLK)

    def shuffle(single, values):
        return jax.random.permutation(single, values)
    kept = jax.vmap(shuffle)(row_keys, kept)
    nearby = jnp.broadcast_to(jnp.array([0, -1, 1], dtype=jnp.int32), (NBLK, 3))
    return jnp.concatenate([nearby, kept], axis=1).astype(jnp.int32)


def draw_columns(key, part):
    offsets = block_offsets(key)
    base = jnp.arange(NBLK, dtype=jnp.int32)[:, None]
    return jnp.mod(base + offsets, NBLK).astype(jnp.int32)


def draw_tiles(key, part):
    offsets = block_offsets(key)
    tile_key = jax.random.fold_in(key, 11)
    spread = (24.0 * BS) ** (-0.5)
    edges = jax.random.normal(tile_key, (NBLK, 4, BS, BS), dtype=jnp.float32) * spread
    base = jnp.arange(NBLK, dtype=jnp.int32)[:, None]
    source = jnp.mod(jnp.where(offsets >= 0, base, base + offsets), NBLK).astype(jnp.int32)
    distance = jnp.abs(offsets).astype(jnp.int32)
    picked = edges[source, distance]
    flipped = jnp.swapaxes(picked, 2, 3)
    upper = jnp.where((offsets > 0)[:, :, None, None], picked, flipped)
    symmetric = (picked + flipped) * 0.5 ** 0.5
    result = jnp.where((offsets == 0)[:, :, None, None], symmetric, upper)
    return result.astype(jnp.bfloat16)


def shard_levels(rng, dims, cuts, smallest, top_value):
    def one(dim, blocks):
        draws = jax.random.uniform(jax.random.fold_in(jax.random.fold_in(rng, 6), dim), (blocks,), jnp.float32, smallest / len(cuts), top_value / len(cuts))
        return jnp.repeat(jnp.exp(draws), dims[dim] // blocks).reshape((-1,) + (1,) * (len(dims) - dim - 1))

    level = one(*cuts[0])
    for cut in cuts[1:]:
        level = level * one(*cut)
    return level


def noise(key, extent, width, most, cuts=(), kind=jnp.bfloat16):
    values = jax.random.normal(key, extent, jnp.float32) * width
    if len(cuts) > 0:
        values = shard_levels(key, extent, cuts, -0.22, 0.18) * values
    return jnp.clip(values, min=-most, max=most).astype(kind)


def setup_inputs(seed: int = 0) -> dict:
    arg_keys = jax.random.split(jax.random.key(seed), 4)
    tiles = draw_tiles(jax.random.fold_in(arg_keys[3], 71), 0)
    columns = draw_columns(jax.random.fold_in(arg_keys[3], 71), 0)
    start_vectors = noise(arg_keys[2], (M, NROW), 1.0, 6.0, ((0, 16), (1, 32)), jnp.float32)
    return dict(tiles=tiles, columns=columns, start_vectors=start_vectors)


def operate(field, tiles32, columns):
    blocked = field.reshape(M, NBLK, BS)

    def one_block(index):
        picked = jnp.take(blocked, columns[index], axis=1)
        return jnp.einsum('mtj,tij->mi', picked, tiles32[index], precision=lax.Precision.HIGHEST)
    outs = lax.map(one_block, jnp.arange(NBLK, dtype=jnp.int32))
    return jnp.transpose(outs, (1, 0, 2)).reshape(M, NBLK * BS)

def reference(tiles, columns, start_vectors):
    tiles32 = tiles.astype(jnp.float32)
    previous = start_vectors
    current = operate(start_vectors, tiles32, columns)
    for step in range(STEPS - 1):
        following = 2.0 * operate(current, tiles32, columns) - previous
        previous = current
        current = following
    gram = jnp.einsum('mn,kn->mk', current, current, precision=lax.Precision.HIGHEST)
    factor = jnp.linalg.cholesky(gram)
    solved = lax.linalg.triangular_solve(factor, current, left_side=True, lower=True)
    return solved * jnp.sqrt(jnp.float32(NBLK * BS))
```

```python
import functools

import jax
import jax.numpy as jnp
from jax import lax
from jax.experimental import pallas as pl
from jax.experimental.pallas import tpu as pltpu
from jax.sharding import PartitionSpec as P

f32, bf16 = jnp.float32, jnp.bfloat16
M, BS, NB, GR = 1024, 128, 8, 8


def split(x):
    hi = x.astype(bf16)
    return hi, (x - hi.astype(f32)).astype(bf16)


def mm(a, b, tb):
    dims = (((1,), (1 if tb else 0,)), ((), ()))
    return lax.dot_general(a, b, dims, preferred_element_type=f32)


def mm3(a, b, tb=False):
    return mm(a[0], b[0], tb) + (mm(a[0], b[1], tb) + mm(a[1], b[0], tb))


def recip(x):
    r = pl.reciprocal(x, approx=True)
    return r * (2.0 - x * r)


def diag_factor(a_ref, w_ref):
    lane = lax.broadcasted_iota(jnp.int32, (8, BS), 1)
    sub = lax.broadcasted_iota(jnp.int32, (8, BS), 0)
    for g in range(BS // GR):
        lo = g * GR
        ing = (lane >= lo) & (lane < lo + GR)
        p = a_ref[lo:lo + 8, :]
        cols = [jnp.broadcast_to(p[:, lo + j:lo + j + 1], (8, BS)) for j in range(GR)]
        x = jnp.where(lane == sub + lo, 1.0, jnp.where(ing, 0.0, p))
        w = x
        for j in range(0, GR, 2):
            cj, ck = cols[j], cols[j + 1]

            def row(v, i):
                return jnp.broadcast_to(v[i:i + 1, :], (8, BS))
            a, b, c = row(cj, j), row(cj, j + 1), row(ck, j + 1)
            det = a * c - b * b
            pair = (sub == j) | (sub == j + 1)
            cjm = jnp.where(sub == j, -1.0, jnp.where(sub == j + 1, 0.0, cj))
            ckm = jnp.where(sub == j + 1, -1.0, jnp.where(sub == j, 0.0, ck))
            r = recip(det)
            x0, x1 = row(x, j), row(x, j + 1)
            y1 = a * x1 - b * x0
            w = jnp.where(sub == j, x0 * lax.rsqrt(a), jnp.where(sub == j + 1, y1 * lax.rsqrt(a * det), w))
            for m in list(range(j + 2, GR)) + [-1]:
                v = x if m < 0 else cols[m]
                v0, v1 = row(v, j), row(v, j + 1)
                y0 = c * v0 - b * v1
                y1 = a * v1 - b * v0
                z = cjm * y0 + ckm * y1
                new = jnp.where(pair, 0.0, v) - r * z
                if m < 0:
                    x = new
                else:
                    cols[m] = new
        w_ref[lo:lo + 8, :] = jnp.where(lane < lo + GR, w, 0.0)
        for h in range(g + 1, BS // GR):
            q = a_ref[h * 8:h * 8 + 8, :]
            cs = [jnp.broadcast_to(q[:, lo + j:lo + j + 1], (8, BS)) for j in range(GR)]
            t = [cs[j] * jnp.broadcast_to(x[j:j + 1, :], (8, BS)) for j in range(GR)]
            while len(t) > 1:
                t = [t[i] + t[i + 1] for i in range(0, len(t), 2)]
            a_ref[h * 8:h * 8 + 8, :] = jnp.where(ing, 0.0, q) - t[0]


def kernel(n_root, v_ref, g_ref, f_ref, o_ref, a_ref, w_ref, whi, wlo, lhi, llo, scol, srow, r_ref, xhi, xlo):
    eye = lax.broadcasted_iota(jnp.int32, (BS, BS), 0) == lax.broadcasted_iota(jnp.int32, (BS, BS), 1)
    for k in range(NB):
        d = jnp.where(eye, g_ref[k * BS:(k + 1) * BS, k * BS:(k + 1) * BS], 0.0)
        srow[:, k * BS:(k + 1) * BS] = jnp.broadcast_to(lax.rsqrt(jnp.sum(d, axis=0, keepdims=True)), (8, BS))
        scol[k * BS:(k + 1) * BS, :] = jnp.broadcast_to(lax.rsqrt(jnp.sum(d, axis=1, keepdims=True)), (BS, BS))

    def column(k):
        s = g_ref[k * BS:, k * BS:(k + 1) * BS] * scol[k * BS:, :] * srow[0:1, k * BS:(k + 1) * BS]
        if k:
            rows = (lhi[k * BS:, :k * BS], llo[k * BS:, :k * BS])
            own = (lhi[k * BS:(k + 1) * BS, :k * BS], llo[k * BS:(k + 1) * BS, :k * BS])
            s = s - mm3(rows, own, True)
        return s

    a_ref[...] = column(0)

    def after(k):
        hi, lo = split(w_ref[...])
        whi[k], wlo[k] = hi, lo
        if k + 1 == NB:
            return
        h, l = split(mm3(split(a_ref[BS:M - k * BS, :]), (hi, lo), True))
        lhi[(k + 1) * BS:, k * BS:(k + 1) * BS] = h
        llo[(k + 1) * BS:, k * BS:(k + 1) * BS] = l
        a_ref[0:M - (k + 1) * BS, :] = column(k + 1)

    def step(k, _):
        diag_factor(a_ref, w_ref)
        for kk in range(NB):
            @pl.when(k == kk)
            def _():
                after(kk)
        return 0
    lax.fori_loop(0, NB, step, 0)
    v = v_ref[0]
    sel = lax.broadcasted_iota(jnp.int32, (64, M), 0) + v * 64 == lax.broadcasted_iota(jnp.int32, (64, M), 1)
    r_ref[...] = jnp.where(sel, f32(n_root), 0.0)
    for k in range(NB - 1, -1, -1):
        cur = mm3(split(r_ref[:, k * BS:(k + 1) * BS]), (whi[k], wlo[k]))
        if k:
            x = split(cur)
            r_ref[:, :k * BS] -= mm3(x, (lhi[k * BS:(k + 1) * BS, :k * BS], llo[k * BS:(k + 1) * BS, :k * BS]))
        h, l = split(cur * srow[0:1, k * BS:(k + 1) * BS])
        xhi[:, k * BS:(k + 1) * BS] = h
        xlo[:, k * BS:(k + 1) * BS] = l
    o_ref[...] = mm3((xhi[...], xlo[...]), split(f_ref[...]))


def k2(v, g, f, n_root=128.0):
    vm = pl.BlockSpec(memory_space=pltpu.VMEM)
    return pl.pallas_call(
        functools.partial(kernel, n_root),
        out_shape=jax.ShapeDtypeStruct((64, 512), f32),
        in_specs=[pl.BlockSpec(memory_space=pltpu.SMEM), vm, vm],
        out_specs=vm,
        scratch_shapes=[
            pltpu.VMEM((M, BS), f32), pltpu.VMEM((BS, BS), f32),
            pltpu.VMEM((NB, BS, BS), bf16), pltpu.VMEM((NB, BS, BS), bf16),
            pltpu.VMEM((M, M), bf16), pltpu.VMEM((M, M), bf16),
            pltpu.VMEM((M, BS), f32), pltpu.VMEM((8, M), f32),
            pltpu.VMEM((64, M), f32), pltpu.VMEM((64, M), bf16), pltpu.VMEM((64, M), bf16)],
        compiler_params=pltpu.CompilerParams(vmem_limit_bytes=48 << 20),
    )(v, g, f)

HB = 3
STEPS = 4


def with_halo(shard, sides, width):
    for axis, dim in sides:
        devices, length = (lax.axis_size(axis), shard.shape[dim])
        up = [(i, (i + 1) % devices) for i in range(devices)]
        down = [(j, i) for i, j in up]
        last = lax.slice_in_dim(shard, length - width, length, axis=dim)
        initial = lax.slice_in_dim(shard, 0, width, axis=dim)
        before = lax.ppermute(last, axis, up)
        after = lax.ppermute(initial, axis, down)
        shard = jnp.concatenate([before, shard, after], axis=dim)
    return shard


def operate(field, band):
    extended = with_halo(field, (("rows", 1),), HB * BS)
    parts = [
        jnp.einsum("mj,ji->mi", extended[:, b * BS:(b + 2 * HB + 1) * BS], band[b], precision=lax.Precision.HIGHEST)
        for b in range(band.shape[0])
    ]
    return jnp.concatenate(parts, axis=1)


def body(tiles, columns, start_vectors):
    blocks_here = tiles.shape[0]
    total_blocks = blocks_here * lax.axis_size("rows")
    first_block = lax.axis_index("rows") * blocks_here
    global_rows = first_block + jnp.arange(blocks_here, dtype=jnp.int32)
    offsets = jnp.mod(columns - global_rows[:, None] + HB, total_blocks)
    chosen = offsets[:, None, :] == jnp.arange(2 * HB + 1, dtype=jnp.int32)[None, :, None]
    tiles32 = jnp.swapaxes(tiles.astype(jnp.float32), 2, 3)
    band = jnp.zeros((blocks_here, 2 * HB + 1, BS, BS), jnp.float32)
    for t in range(tiles.shape[1]):
        band = band + jnp.where(chosen[:, :, t, None, None], tiles32[:, None, t], 0.0)
    band = band.reshape(blocks_here, (2 * HB + 1) * BS, BS)
    previous = start_vectors
    current = operate(start_vectors, band)
    for step in range(STEPS - 1):
        following = 2.0 * operate(current, band) - previous
        previous = current
        current = following
    width = current.shape[0]
    gathered = lax.all_gather(current, "vecs", axis=0, tiled=True)
    partial_rows = jnp.einsum("mn,kn->mk", current, gathered, precision=lax.Precision.HIGHEST)
    summed_rows = lax.psum(partial_rows, "rows")
    gram = lax.all_gather(summed_rows, "vecs", axis=0, tiled=True)
    where = lax.axis_index("vecs").astype(jnp.int32).reshape(1)
    return k2(where, gram, gathered)


def solution(mesh):
    placed = (P("rows", None, None, None), P("rows", None), P("vecs", "rows"))
    return jax.shard_map(
        body, mesh=mesh, in_specs=placed, out_specs=P("vecs", "rows"), check_vma=False
    )
```

```python
import functools

import jax
import jax.numpy as jnp
from jax import lax
from jax.experimental import pallas as pl
from jax.experimental.pallas import tpu as pltpu
from jax.sharding import PartitionSpec as P

f32, bf16 = jnp.float32, jnp.bfloat16
M, BS, NB, GR = 1024, 128, 8, 8


def split(x):
    hi = x.astype(bf16)
    return hi, (x - hi.astype(f32)).astype(bf16)


def mm(a, b, tb):
    dims = (((1,), (1 if tb else 0,)), ((), ()))
    return lax.dot_general(a, b, dims, preferred_element_type=f32)


def mm3(a, b, tb=False):
    return mm(a[0], b[0], tb) + (mm(a[0], b[1], tb) + mm(a[1], b[0], tb))


def recip(x):
    r = pl.reciprocal(x, approx=True)
    return r * (2.0 - x * r)


def diag_factor(a_ref, w_ref):
    lane = lax.broadcasted_iota(jnp.int32, (8, BS), 1)
    sub = lax.broadcasted_iota(jnp.int32, (8, BS), 0)
    for g in range(BS // GR):
        lo = g * GR
        ing = (lane >= lo) & (lane < lo + GR)
        p = a_ref[lo:lo + 8, :]
        cols = [jnp.broadcast_to(p[:, lo + j:lo + j + 1], (8, BS)) for j in range(GR)]
        x = jnp.where(lane == sub + lo, 1.0, jnp.where(ing, 0.0, p))
        w = x
        for j in range(0, GR, 2):
            cj, ck = cols[j], cols[j + 1]

            def row(v, i):
                return jnp.broadcast_to(v[i:i + 1, :], (8, BS))
            a, b, c = row(cj, j), row(cj, j + 1), row(ck, j + 1)
            det = a * c - b * b
            pair = (sub == j) | (sub == j + 1)
            cjm = jnp.where(sub == j, -1.0, jnp.where(sub == j + 1, 0.0, cj))
            ckm = jnp.where(sub == j + 1, -1.0, jnp.where(sub == j, 0.0, ck))
            r = recip(det)
            x0, x1 = row(x, j), row(x, j + 1)
            y1 = a * x1 - b * x0
            w = jnp.where(sub == j, x0 * lax.rsqrt(a), jnp.where(sub == j + 1, y1 * lax.rsqrt(a * det), w))
            for m in list(range(j + 2, GR)) + [-1]:
                v = x if m < 0 else cols[m]
                v0, v1 = row(v, j), row(v, j + 1)
                y0 = c * v0 - b * v1
                y1 = a * v1 - b * v0
                z = cjm * y0 + ckm * y1
                new = jnp.where(pair, 0.0, v) - r * z
                if m < 0:
                    x = new
                else:
                    cols[m] = new
        w_ref[lo:lo + 8, :] = jnp.where(lane < lo + GR, w, 0.0)
        for h in range(g + 1, BS // GR):
            q = a_ref[h * 8:h * 8 + 8, :]
            cs = [jnp.broadcast_to(q[:, lo + j:lo + j + 1], (8, BS)) for j in range(GR)]
            t = [cs[j] * jnp.broadcast_to(x[j:j + 1, :], (8, BS)) for j in range(GR)]
            while len(t) > 1:
                t = [t[i] + t[i + 1] for i in range(0, len(t), 2)]
            a_ref[h * 8:h * 8 + 8, :] = jnp.where(ing, 0.0, q) - t[0]


def kernel(n_root, v_ref, g_ref, f_ref, o_ref, a_ref, w_ref, whi, wlo, lhi, llo, scol, srow, r_ref, xhi, xlo):
    def block(i, j):
        d = i - j
        if d <= 4:
            return g_ref[2 * i:2 * i + 2, d].reshape(BS, BS)
        return g_ref[2 * j:2 * j + 2, NB - d].reshape(BS, BS).T

    eye = lax.broadcasted_iota(jnp.int32, (BS, BS), 0) == lax.broadcasted_iota(jnp.int32, (BS, BS), 1)
    for k in range(NB):
        d = jnp.where(eye, block(k, k), 0.0)
        srow[:, k * BS:(k + 1) * BS] = jnp.broadcast_to(lax.rsqrt(jnp.sum(d, axis=0, keepdims=True)), (8, BS))
        scol[k * BS:(k + 1) * BS, :] = jnp.broadcast_to(lax.rsqrt(jnp.sum(d, axis=1, keepdims=True)), (BS, BS))

    def column(k):
        s = jnp.concatenate([block(i, k) for i in range(k, NB)], axis=0) * scol[k * BS:, :] * srow[0:1, k * BS:(k + 1) * BS]
        if k:
            rows = (lhi[k * BS:, :k * BS], llo[k * BS:, :k * BS])
            own = (lhi[k * BS:(k + 1) * BS, :k * BS], llo[k * BS:(k + 1) * BS, :k * BS])
            s = s - mm3(rows, own, True)
        return s

    a_ref[...] = column(0)

    def after(k):
        hi, lo = split(w_ref[...])
        whi[k], wlo[k] = hi, lo
        if k + 1 == NB:
            return
        h, l = split(mm3(split(a_ref[BS:M - k * BS, :]), (hi, lo), True))
        lhi[(k + 1) * BS:, k * BS:(k + 1) * BS] = h
        llo[(k + 1) * BS:, k * BS:(k + 1) * BS] = l
        a_ref[0:M - (k + 1) * BS, :] = column(k + 1)

    def step(k, _):
        diag_factor(a_ref, w_ref)
        for kk in range(NB):
            @pl.when(k == kk)
            def _():
                after(kk)
        return 0
    lax.fori_loop(0, NB, step, 0)
    v = v_ref[0]
    sel = lax.broadcasted_iota(jnp.int32, (64, M), 0) + v * 64 == lax.broadcasted_iota(jnp.int32, (64, M), 1)
    r_ref[...] = jnp.where(sel, f32(n_root), 0.0)
    for k in range(NB - 1, -1, -1):
        cur = mm3(split(r_ref[:, k * BS:(k + 1) * BS]), (whi[k], wlo[k]))
        if k:
            x = split(cur)
            r_ref[:, :k * BS] -= mm3(x, (lhi[k * BS:(k + 1) * BS, :k * BS], llo[k * BS:(k + 1) * BS, :k * BS]))
        h, l = split(cur * srow[0:1, k * BS:(k + 1) * BS])
        xhi[:, k * BS:(k + 1) * BS] = h
        xlo[:, k * BS:(k + 1) * BS] = l
    o_ref[...] = mm3((xhi[...], xlo[...]), split(f_ref[...].reshape(M, 512)))


def k2(v, g, f, n_root=128.0):
    vm = pl.BlockSpec(memory_space=pltpu.VMEM)
    return pl.pallas_call(
        functools.partial(kernel, n_root),
        out_shape=jax.ShapeDtypeStruct((64, 512), f32),
        in_specs=[pl.BlockSpec(memory_space=pltpu.SMEM), vm, vm],
        out_specs=vm,
        scratch_shapes=[
            pltpu.VMEM((M, BS), f32), pltpu.VMEM((BS, BS), f32),
            pltpu.VMEM((NB, BS, BS), bf16), pltpu.VMEM((NB, BS, BS), bf16),
            pltpu.VMEM((M, M), bf16), pltpu.VMEM((M, M), bf16),
            pltpu.VMEM((M, BS), f32), pltpu.VMEM((8, M), f32),
            pltpu.VMEM((64, M), f32), pltpu.VMEM((64, M), bf16), pltpu.VMEM((64, M), bf16)],
        compiler_params=pltpu.CompilerParams(vmem_limit_bytes=48 << 20),
    )(v, g, f)


MESH = pl.DeviceIdType.MESH
NR, NY, ND, NQ = 32, 8, 5, 20
HALO, W = 384, 512


def device_of(q):
    return (q * 8) // 5


def k1_kernel(columns_ref, tiles_ref, y0_ref, f_out, g_out, wt, ys, hl, hr, gath, gb, part, inbox,
              hs, hrl, hrr, fs, fr, gs, gr, ds, dr, es, er, out_sem):
    r, v = lax.axis_index("rows"), lax.axis_index("vecs")
    y, c = v // 2, v % 2
    sib, yr, yl = y * 2 + 1 - c, lax.rem(y + 1, NY) * 2 + c, lax.rem(y + NY - 1, NY) * 2 + c
    right, left = lax.rem(r + 1, NR), lax.rem(r + NR - 1, NR)

    barrier = pltpu.get_barrier_semaphore()

    def greet(d, _):
        pl.semaphore_signal(barrier, inc=1, device_id=(lax.rem(r + d, NR), v), device_id_type=MESH)
        return 0
    lax.fori_loop(1, NR, greet, 0)
    for other in (sib, yr, yl):
        pl.semaphore_signal(barrier, inc=1, device_id=(r, other), device_id_type=MESH)

    def rcopy(src, dst, send, recv, to):
        return pltpu.make_async_remote_copy(src_ref=src, dst_ref=dst, send_sem=send, recv_sem=recv, device_id=to, device_id_type=MESH)

    wt[...] = jnp.zeros_like(wt)
    for b in range(4):
        rows = slice(b * BS, (b + 1) * BS)
        for t, o in ((0, 0), (1, -1), (2, 1)):
            wt[rows, (b + 3 + o) * BS:(b + 4 + o) * BS] = tiles_ref[b, t]
        for o in (-3, -2, 2, 3):
            want = lax.rem(r * 4 + b + o + 4 * NR, 4 * NR)
            tile = jnp.zeros((BS, BS), bf16)
            for t in (3, 4, 5):
                tile = jnp.where(columns_ref[b, t] == want, tiles_ref[b, t], tile)
            wt[rows, (b + 3 + o) * BS:(b + 4 + o) * BS] = tile

    pl.semaphore_wait(barrier, NR - 1 + 3)

    def stacked(x):
        return jnp.concatenate(split(x), axis=0)

    def halves(x):
        return x[:64] + x[64:]

    waits = []
    for s in range(4):
        src = y0_ref if s == 0 else ys.at[s - 1]
        to_right = rcopy(src.at[:, W - HALO:], hl.at[s], hs.at[2 * s], hrl.at[s], (right, v))
        to_left = rcopy(src.at[:, :HALO], hr.at[s], hs.at[2 * s + 1], hrr.at[s], (left, v))
        to_right.start()
        to_left.start()
        waits += [to_right, to_left]
        cur = src[...]
        acc = halves(mm(stacked(cur), wt[:, HALO:HALO + W], True))
        if s == 1:
            prev = y0_ref[...]
        elif s > 1:
            prev = ys[s - 2]
        to_right.wait_recv()
        wl = halves(mm(stacked(hl[s]), wt[:HALO, :HALO], True))
        to_left.wait_recv()
        wr = halves(mm(stacked(hr[s]), wt[BS:, HALO + W:], True))
        parts = [acc[:, :BS] + wl[:, :BS], acc[:, BS:HALO] + wl[:, BS:] + wr[:, :2 * BS], acc[:, HALO:] + wr[:, 2 * BS:]]
        new = jnp.concatenate(parts, axis=1)
        if s:
            new = 2.0 * new - prev
        if s < 3:
            ys[s] = new
        else:
            gath[v] = new

    def ring(buf, cut, send, recv, each):
        def slot(d):
            return lax.rem(y + NY + d, NY) * 2 + c

        def other(d):
            return lax.rem(y + NY + d, NY) * 2 + 1 - c

        def block(i, part=None):
            return buf.at[i] if part is None else buf.at[i, part]
        lo, hi = pl.ds(0, cut), pl.ds(cut, cut)

        def go(i, n, to, part=None):
            k = rcopy(block(i, part), block(i, part), send.at[n], recv.at[n], (r, to))
            k.start()
            waits.append(k)

        def arrive(i, n, part=None):
            rcopy(block(i, part), block(i, part), send.at[n], recv.at[n], (r, sib)).wait_recv()
        go(v, 0, yr)
        go(v, 4, yl)
        go(v, 11, sib)
        for s in range(1, 4):
            p, q = (lo, hi) if s == 3 else (None, None)
            arrive(slot(-s), s - 1)
            go(slot(-s), s, yr, p)
            go(slot(-s), 11 - s, sib)
            arrive(slot(s), 3 + s)
            go(slot(s), 4 + s, yl, q)
            go(slot(s), 11 + s, sib)
            if s == 1:
                arrive(other(0), 11)
            else:
                arrive(other(1 - s), 12 - s)
            each(1 - s)
        arrive(other(-3), 8)
        each(-3)
        arrive(slot(4), 3, lo)
        go(slot(4), 15, sib, lo)
        arrive(slot(4), 7, hi)
        go(slot(4), 16, sib, hi)
        arrive(other(4), 15, lo)
        arrive(other(4), 16, hi)
        each(-4)
        for d in (1, 2, 3):
            arrive(other(d), 11 + d)

    own = split(gath[v])

    def gram_part(d):
        at = lax.rem(y + NY + d, NY)
        pair = split(gath[pl.ds(at * 2, 2)].reshape(BS, W))
        g = mm3(own, pair, True)
        for t in range(4):
            q = -d * 4 + t
            part[q] = g[t * 16:(t + 1) * 16]
            to = device_of(q)
            rel = lax.rem(r - to + NR, NR)

            @pl.when(r != to)
            def _():
                rcopy(part.at[q], inbox.at[rel], ds.at[q], dr.at[rel], (to, v)).start()

    ring(gath, 32, fs, fr, gram_part)
    f_copy = pltpu.make_async_copy(gath, f_out, out_sem.at[0])
    f_copy.start()

    z = r % 8
    zq = (z * 5 + 4) // 8
    mine = (r // 8) * 5 + zq
    active = (zq * 8) // 5 == z

    @pl.when(active)
    def _():
        def add(rel, total):
            rcopy(part.at[0], inbox.at[rel], ds.at[0], dr.at[rel], (right, v)).wait_recv()
            return total + inbox[rel]
        gb[v, mine] = lax.fori_loop(1, NR, add, part[mine])

        def send(rel, _):
            rcopy(gb.at[v, mine], gb.at[v, mine], es.at[rel], er.at[mine], (lax.rem(r + rel, NR), v)).start()
            return 0
        lax.fori_loop(1, NR, send, 0)
    for q in range(NQ):
        @pl.when(r != device_of(q))
        def _():
            rcopy(gb.at[v, q], gb.at[v, q], es.at[0], er.at[q], (right, v)).wait_recv()

    ring(gb, NQ // 2, gs, gr, lambda d: None)
    g_copy = pltpu.make_async_copy(gb, g_out, out_sem.at[1])
    g_copy.start()
    for k in waits:
        k.wait_send()
    for q in range(NQ):
        @pl.when(r != device_of(q))
        def _():
            rcopy(part.at[q], inbox.at[0], ds.at[q], dr.at[0], (right, v)).wait_send()

    @pl.when(active)
    def _():
        def done(rel, _):
            rcopy(gb.at[v, mine], gb.at[v, mine], es.at[rel], er.at[mine], (right, v)).wait_send()
            return 0
        lax.fori_loop(1, NR, done, 0)
    f_copy.wait()
    g_copy.wait()


def k1(tiles, columns, start):
    vm = pl.BlockSpec(memory_space=pltpu.VMEM)
    dma = pltpu.SemaphoreType.DMA
    return pl.pallas_call(
        k1_kernel,
        out_shape=(jax.ShapeDtypeStruct((16, 64, W), f32), jax.ShapeDtypeStruct((16, NQ, 16, BS), f32)),
        in_specs=[pl.BlockSpec(memory_space=pltpu.SMEM), vm, vm],
        out_specs=(pl.BlockSpec(memory_space=pl.ANY), pl.BlockSpec(memory_space=pl.ANY)),
        scratch_shapes=[
            pltpu.VMEM((W, W + 2 * HALO), bf16), pltpu.VMEM((3, 64, W), f32),
            pltpu.VMEM((4, 64, HALO), f32), pltpu.VMEM((4, 64, HALO), f32),
            pltpu.VMEM((16, 64, W), f32), pltpu.VMEM((16, NQ, 16, BS), f32),
            pltpu.VMEM((NQ, 16, BS), f32), pltpu.VMEM((NR, 16, BS), f32),
            dma((8,)), dma((4,)), dma((4,)), dma((17,)), dma((17,)), dma((17,)), dma((17,)),
            dma((NQ,)), dma((NR,)), dma((NR,)), dma((NQ,)), dma((2,))],
        compiler_params=pltpu.CompilerParams(collective_id=0, has_side_effects=True, vmem_limit_bytes=32 << 20),
    )(columns, tiles, start)


def body(tiles, columns, start_vectors):
    gathered, gram = k1(tiles, columns, start_vectors)
    where = lax.axis_index("vecs").astype(jnp.int32).reshape(1)
    return k2(where, gram.reshape(16, ND, 64, BS), gathered)


def solution(mesh):
    placed = (P("rows", None, None, None), P("rows", None), P("vecs", "rows"))
    return jax.shard_map(
        body, mesh=mesh, in_specs=placed, out_specs=P("vecs", "rows"), check_vma=False
    )
```

```python
import functools

import jax
import jax.numpy as jnp
from jax import lax
from jax.experimental import pallas as pl
from jax.experimental.pallas import tpu as pltpu
from jax.sharding import PartitionSpec as P

f32, bf16 = jnp.float32, jnp.bfloat16
M, BS, NB, GR = 1024, 128, 8, 8
MESH = pl.DeviceIdType.MESH
NR, NY, ND, NQ = 32, 8, 5, 20
HALO, W, HALF = 384, 512, 32


def split(x):
    hi = x.astype(bf16)
    return hi, (x - hi.astype(f32)).astype(bf16)


def mm(a, b, tb):
    dims = (((1,), (1 if tb else 0,)), ((), ()))
    return lax.dot_general(a, b, dims, preferred_element_type=f32)


def mm3(a, b, tb=False):
    return mm(a[0], b[0], tb) + (mm(a[0], b[1], tb) + mm(a[1], b[0], tb))


def recip(x):
    r = pl.reciprocal(x, approx=True)
    return r * (2.0 - x * r)


def diag_factor(a_ref, w_ref, srow_ref):
    full = a_ref[:BS, :]
    eye = lax.broadcasted_iota(jnp.int32, (BS, BS), 0) == lax.broadcasted_iota(jnp.int32, (BS, BS), 1)
    only = jnp.where(eye, full, 0.0)
    srow = lax.rsqrt(jnp.sum(only, axis=0, keepdims=True))
    srow_ref[...] = jnp.broadcast_to(srow, (8, BS))
    a_ref[:BS, :] = full * srow * lax.rsqrt(jnp.sum(only, axis=1, keepdims=True))
    lane = lax.broadcasted_iota(jnp.int32, (8, BS), 1)
    sub = lax.broadcasted_iota(jnp.int32, (8, BS), 0)
    for g in range(BS // GR):
        lo = g * GR
        ing = (lane >= lo) & (lane < lo + GR)
        p = a_ref[lo:lo + 8, :]
        cols = [jnp.broadcast_to(p[:, lo + j:lo + j + 1], (8, BS)) for j in range(GR)]
        x = jnp.where(lane == sub + lo, 1.0, jnp.where(ing, 0.0, p))
        w = x
        for j in range(0, GR, 2):
            cj, ck = cols[j], cols[j + 1]

            def row(v, i):
                return jnp.broadcast_to(v[i:i + 1, :], (8, BS))
            a, b, c = row(cj, j), row(cj, j + 1), row(ck, j + 1)
            det = a * c - b * b
            pair = (sub == j) | (sub == j + 1)
            cjm = jnp.where(sub == j, -1.0, jnp.where(sub == j + 1, 0.0, cj))
            ckm = jnp.where(sub == j + 1, -1.0, jnp.where(sub == j, 0.0, ck))
            r = recip(det)
            x0, x1 = row(x, j), row(x, j + 1)
            y1 = a * x1 - b * x0
            w = jnp.where(sub == j, x0 * lax.rsqrt(a), jnp.where(sub == j + 1, y1 * lax.rsqrt(a * det), w))
            for m in list(range(j + 2, GR)) + [-1]:
                v = x if m < 0 else cols[m]
                v0, v1 = row(v, j), row(v, j + 1)
                y0 = c * v0 - b * v1
                y1 = a * v1 - b * v0
                z = cjm * y0 + ckm * y1
                new = jnp.where(pair, 0.0, v) - r * z
                if m < 0:
                    x = new
                else:
                    cols[m] = new
        w_ref[lo:lo + 8, :] = jnp.where(lane < lo + GR, w, 0.0)
        for h in range(g + 1, BS // GR):
            q = a_ref[h * 8:h * 8 + 8, :]
            cs = [jnp.broadcast_to(q[:, lo + j:lo + j + 1], (8, BS)) for j in range(GR)]
            t = [cs[j] * jnp.broadcast_to(x[j:j + 1, :], (8, BS)) for j in range(GR)]
            while len(t) > 1:
                t = [t[i] + t[i + 1] for i in range(0, len(t), 2)]
            a_ref[h * 8:h * 8 + 8, :] = jnp.where(ing, 0.0, q) - t[0]


def device_of(q):
    return (q * 8) // 5


def transfers(k):
    return [(i, i - k) for i in range(k, min(k + 5, NB))] + [(k, d) for d in range(k + 1, 4)]


def kernel(n_root, columns_ref, tiles_ref, y0_ref, o_ref, wt, ys, hl, hr, gath, gb, part, inbox,
           a_ref, w_ref, srow, whi, wlo, lhi, llo, r_ref, xhi, xlo,
           hs, hrl, hrr, fs, fr, ds, dr, es, er, ts, tr, tf, tb):
    r, v = lax.axis_index("rows"), lax.axis_index("vecs")
    y, c = v // 2, v % 2
    sib, yr, yl = y * 2 + 1 - c, lax.rem(y + 1, NY) * 2 + c, lax.rem(y + NY - 1, NY) * 2 + c
    right, left = lax.rem(r + 1, NR), lax.rem(r + NR - 1, NR)

    barrier = pltpu.get_barrier_semaphore()

    def greet(d, _):
        pl.semaphore_signal(barrier, inc=1, device_id=(lax.rem(r + d, NR), v), device_id_type=MESH)
        return 0
    lax.fori_loop(1, NR, greet, 0)

    def greet_y(d, _):
        pl.semaphore_signal(barrier, inc=1, device_id=(r, lax.rem(y + d, NY) * 2 + c), device_id_type=MESH)
        return 0
    lax.fori_loop(1, NY, greet_y, 0)
    pl.semaphore_signal(barrier, inc=1, device_id=(r, sib), device_id_type=MESH)

    def rcopy(src, dst, send, recv, to):
        return pltpu.make_async_remote_copy(src_ref=src, dst_ref=dst, send_sem=send, recv_sem=recv, device_id=to, device_id_type=MESH)

    wt[...] = jnp.zeros_like(wt)
    for b in range(4):
        rows = slice(b * BS, (b + 1) * BS)
        for t, o in ((0, 0), (1, -1), (2, 1)):
            wt[rows, (b + 3 + o) * BS:(b + 4 + o) * BS] = tiles_ref[b, t]
        for o in (-3, -2, 2, 3):
            want = lax.rem(r * 4 + b + o + 4 * NR, 4 * NR)
            tile = jnp.zeros((BS, BS), bf16)
            for t in (3, 4, 5):
                tile = jnp.where(columns_ref[b, t] == want, tiles_ref[b, t], tile)
            wt[rows, (b + 3 + o) * BS:(b + 4 + o) * BS] = tile

    pl.semaphore_wait(barrier, NR - 1 + NY - 1 + 1)

    def stacked(x):
        return jnp.concatenate(split(x), axis=0)

    def halves(x):
        n = x.shape[0] // 2
        return x[:n] + x[n:]

    waits = []
    rows_of = (slice(0, HALF), slice(HALF, 2 * HALF))

    def field(s):
        return y0_ref if s == 0 else ys.at[s - 1]

    def halo(s, h, go):
        src, n = field(s), 2 * s + h
        to_right = rcopy(src.at[rows_of[h], W - HALO:], hl.at[s, rows_of[h]], hs.at[2 * n], hrl.at[n], (right, v))
        to_left = rcopy(src.at[rows_of[h], :HALO], hr.at[s, rows_of[h]], hs.at[2 * n + 1], hrr.at[n], (left, v))
        if go:
            to_right.start()
            to_left.start()
            waits.extend((to_right, to_left))
        else:
            to_right.wait_recv()
            to_left.wait_recv()

    def slot(d):
        return lax.rem(y + NY + d, NY) * 2 + c

    def other(d):
        return lax.rem(y + NY + d, NY) * 2 + 1 - c

    def half(i, h):
        return gath.at[i, rows_of[h]]

    def go(i, n, h, to):
        k = rcopy(half(i, h), half(i, h), fs.at[2 * n + h], fr.at[2 * n + h], (r, to))
        k.start()
        waits.append(k)

    def arrive(i, n, h):
        rcopy(half(i, h), half(i, h), fs.at[2 * n + h], fr.at[2 * n + h], (r, sib)).wait_recv()

    halo(0, 0, True)
    halo(0, 1, True)
    for s in range(4):
        acc = halves(mm(stacked(field(s)[...]), wt[:, HALO:HALO + W], True))
        for h in range(2):
            rows = rows_of[h]
            halo(s, h, False)
            wl = halves(mm(stacked(hl[s, rows]), wt[:HALO, :HALO], True))
            wr = halves(mm(stacked(hr[s, rows]), wt[BS:, HALO + W:], True))
            mid = acc[rows]
            parts = [mid[:, :BS] + wl[:, :BS], mid[:, BS:HALO] + wl[:, BS:] + wr[:, :2 * BS], mid[:, HALO:] + wr[:, 2 * BS:]]
            new = jnp.concatenate(parts, axis=1)
            if s:
                new = 2.0 * new - field(s - 1)[rows]
            if s < 3:
                ys[s, rows] = new
                halo(s + 1, h, True)
            else:
                gath[v, rows] = new
                go(v, 0, h, yr)
                go(v, 4, h, yl)
                go(v, 11, h, sib)

    own = split(gath[v])

    def gram_part(d):
        at = lax.rem(y + NY - d, NY)
        pair = split(gath[pl.ds(at * 2, 2)].reshape(BS, W))
        g = mm3(own, pair, True)
        for t in range(4):
            q = d * 4 + t
            part[q] = g[t * 16:(t + 1) * 16]
            to = device_of(q)
            rel = lax.rem(r - to + NR, NR)

            @pl.when(r != to)
            def _():
                rcopy(part.at[q], inbox.at[rel], ds.at[q], dr.at[rel], (to, v)).start()

    for s in range(1, 4):
        for h in range(2):
            arrive(slot(-s), s - 1, h)
            if s < 3 or h == 0:
                go(slot(-s), s, h, yr)
            go(slot(-s), 11 - s, h, sib)
            arrive(slot(s), 3 + s, h)
            if s < 3 or h == 1:
                go(slot(s), 4 + s, h, yl)
            go(slot(s), 11 + s, h, sib)
        for h in range(2):
            arrive(other(1 - s), 12 - s, h)
        gram_part(s - 1)
    for h in range(2):
        arrive(other(-3), 8, h)
    gram_part(3)
    arrive(slot(4), 3, 0)
    go(slot(4), 15, 0, sib)
    arrive(slot(4), 7, 1)
    go(slot(4), 15, 1, sib)
    arrive(other(4), 15, 0)
    arrive(other(4), 15, 1)
    gram_part(4)

    z = r % 8
    zq = (z * 5 + 4) // 8
    mine = (r // 8) * 5 + zq
    active = (zq * 8) // 5 == z

    @pl.when(active)
    def _():
        def add(rel, total):
            rcopy(part.at[0], inbox.at[rel], ds.at[0], dr.at[rel], (right, v)).wait_recv()
            return total + inbox[rel]
        gb[v, mine] = lax.fori_loop(1, NR, add, part[mine])

        def send(rel, _):
            rcopy(gb.at[v, mine], gb.at[v, mine], es.at[rel], er.at[mine], (lax.rem(r + rel, NR), v)).start()
            return 0
        lax.fori_loop(1, NR, send, 0)
    for q in range(NQ):
        @pl.when(r != device_of(q))
        def _():
            rcopy(gb.at[v, q], gb.at[v, q], es.at[0], er.at[q], (right, v)).wait_recv()

    def piece(i, d, core):
        return gb.at[i * 2 + core, 4 * d:4 * d + 4]

    def send_block(i, d):
        @pl.when(y == i)
        def _():
            rcopy(piece(i, d, c), piece(i, d, c), ts.at[8 * d], tb.at[5 * i + d], (r, sib)).start()

            def one(n, _):
                rcopy(piece(i, d, c), piece(i, d, c), ts.at[8 * d + n], tr.at[5 * i + d], (r, lax.rem(y + n, NY) * 2 + c)).start()
                return 0
            lax.fori_loop(1, NY, one, 0)

    def pass_block(i, d):
        @pl.when(y != i)
        def _():
            rcopy(piece(i, d, c), piece(i, d, c), ts.at[0], tr.at[5 * i + d], (r, sib)).wait_recv()
            rcopy(piece(i, d, c), piece(i, d, c), tf.at[5 * i + d], tb.at[5 * i + d], (r, sib)).start()

    def take_block(i, d):
        rcopy(piece(i, d, 1 - c), piece(i, d, 1 - c), ts.at[0], tb.at[5 * i + d], (r, sib)).wait_recv()

    def block(i, j):
        d = i - j
        if d <= 4:
            return gb[2 * i:2 * i + 2, 4 * d:4 * d + 4].reshape(BS, BS)
        d = NB - d
        return gb[2 * j:2 * j + 2, 4 * d:4 * d + 4].reshape(BS, BS).T

    def column(k):
        s = jnp.concatenate([block(i, k) for i in range(k, NB)], axis=0)
        if k:
            rows = (lhi[k * BS:, :k * BS], llo[k * BS:, :k * BS])
            own = (lhi[k * BS:(k + 1) * BS, :k * BS], llo[k * BS:(k + 1) * BS, :k * BS])
            s = s - mm3(rows, own, True)
        return s

    for i, d in transfers(0) + transfers(1):
        send_block(i, d)
    pass_block(0, 0)
    take_block(0, 0)
    a_ref[:BS, :] = block(0, 0)

    def after(k):
        hi, lo = split(w_ref[...] * srow[0:1, :])
        whi[k], wlo[k] = hi, lo
        if k + 1 == NB:
            return
        if k + 2 < NB:
            for i, d in transfers(k + 2):
                send_block(i, d)
        todo = (transfers(0)[1:] if k == 0 else []) + transfers(k + 1)
        for i, d in todo:
            pass_block(i, d)
        for i, d in todo:
            take_block(i, d)
        if k == 0:
            a_ref[BS:, :] = column(0)[BS:]
        h, l = split(mm3(split(a_ref[BS:M - k * BS, :]), (hi, lo), True))
        lhi[(k + 1) * BS:, k * BS:(k + 1) * BS] = h
        llo[(k + 1) * BS:, k * BS:(k + 1) * BS] = l
        a_ref[0:M - (k + 1) * BS, :] = column(k + 1)

    def step(k, _):
        diag_factor(a_ref, w_ref, srow)
        for kk in range(NB):
            @pl.when(k == kk)
            def _():
                after(kk)
        return 0
    lax.fori_loop(0, NB, step, 0)

    sel = lax.broadcasted_iota(jnp.int32, (64, M), 0) + v * 64 == lax.broadcasted_iota(jnp.int32, (64, M), 1)
    r_ref[...] = jnp.where(sel, f32(n_root), 0.0)
    for k in range(NB - 1, -1, -1):
        x = split(mm3(split(r_ref[:, k * BS:(k + 1) * BS]), (whi[k], wlo[k])))
        if k:
            r_ref[:, :k * BS] -= mm3(x, (lhi[k * BS:(k + 1) * BS, :k * BS], llo[k * BS:(k + 1) * BS, :k * BS]))
        xhi[:, k * BS:(k + 1) * BS] = x[0]
        xlo[:, k * BS:(k + 1) * BS] = x[1]
    for d in (1, 2, 3):
        for h in range(2):
            arrive(other(d), 11 + d, h)
    o_ref[...] = mm3((xhi[...], xlo[...]), split(gath[...].reshape(M, W)))

    for k in waits:
        k.wait_send()
    for q in range(NQ):
        @pl.when(r != device_of(q))
        def _():
            rcopy(part.at[q], inbox.at[0], ds.at[q], dr.at[0], (right, v)).wait_send()

    @pl.when(active)
    def _():
        def done(rel, _):
            rcopy(gb.at[v, mine], gb.at[v, mine], es.at[rel], er.at[mine], (right, v)).wait_send()
            return 0
        lax.fori_loop(1, NR, done, 0)

    def sent(n, _):
        rcopy(piece(0, 0, c), piece(0, 0, c), ts.at[n], tr.at[0], (r, sib)).wait_send()
        return 0
    lax.fori_loop(0, 32, sent, 0)

    @pl.when(y >= 4)
    def _():
        lax.fori_loop(32, 40, sent, 0)
    for k in range(NB):
        for i, d in transfers(k):
            @pl.when(y != i)
            def _():
                rcopy(piece(i, d, c), piece(i, d, c), tf.at[5 * i + d], tb.at[5 * i + d], (r, sib)).wait_send()


def solve(tiles, columns, start, n_root=128.0):
    vm = pl.BlockSpec(memory_space=pltpu.VMEM)
    dma = pltpu.SemaphoreType.DMA
    return pl.pallas_call(
        functools.partial(kernel, n_root),
        out_shape=jax.ShapeDtypeStruct((64, W), f32),
        in_specs=[pl.BlockSpec(memory_space=pltpu.SMEM), vm, vm],
        out_specs=vm,
        scratch_shapes=[
            pltpu.VMEM((W, W + 2 * HALO), bf16), pltpu.VMEM((3, 64, W), f32),
            pltpu.VMEM((4, 64, HALO), f32), pltpu.VMEM((4, 64, HALO), f32),
            pltpu.VMEM((16, 64, W), f32), pltpu.VMEM((16, NQ, 16, BS), f32),
            pltpu.VMEM((NQ, 16, BS), f32), pltpu.VMEM((NR, 16, BS), f32),
            pltpu.VMEM((M, BS), f32), pltpu.VMEM((BS, BS), f32), pltpu.VMEM((8, BS), f32),
            pltpu.VMEM((NB, BS, BS), bf16), pltpu.VMEM((NB, BS, BS), bf16),
            pltpu.VMEM((M, M), bf16), pltpu.VMEM((M, M), bf16),
            pltpu.VMEM((64, M), f32), pltpu.VMEM((64, M), bf16), pltpu.VMEM((64, M), bf16),
            dma((16,)), dma((8,)), dma((8,)), dma((32,)), dma((32,)),
            dma((NQ,)), dma((NR,)), dma((NR,)), dma((NQ,)),
            dma((40,)), dma((40,)), dma((40,)), dma((40,))],
        compiler_params=pltpu.CompilerParams(collective_id=0, has_side_effects=True, vmem_limit_bytes=48 << 20),
    )(columns, tiles, start)


def solution(mesh):
    placed = (P("rows", None, None, None), P("rows", None), P("vecs", "rows"))
    return jax.shard_map(
        solve, mesh=mesh, in_specs=placed, out_specs=P("vecs", "rows"), check_vma=False
    )
```

```python
import functools
import types

import jax
import jax.numpy as jnp
from jax import lax
from jax.experimental import pallas as pl
from jax.experimental.pallas import tpu as pltpu
from jax.sharding import PartitionSpec as P

f32, bf16 = jnp.float32, jnp.bfloat16
M, BS, NB, GR = 1024, 128, 8, 8
MESH = pl.DeviceIdType.MESH
NR, NY, ND, NQ = 32, 8, 5, 20
HALO, W, HALF = 384, 512, 32


def split(x):
    hi = x.astype(bf16)
    return hi, (x - hi.astype(f32)).astype(bf16)


def mm(a, b, tb):
    dims = (((1,), (1 if tb else 0,)), ((), ()))
    return lax.dot_general(a, b, dims, preferred_element_type=f32)


def mm3(a, b, tb=False):
    return mm(a[0], b[0], tb) + (mm(a[0], b[1], tb) + mm(a[1], b[0], tb))


def recip(x):
    r = pl.reciprocal(x, approx=True)
    return r * (2.0 - x * r)


def diag_factor(a_ref, w_ref, srow_ref):
    full = a_ref[:BS, :]
    eye = lax.broadcasted_iota(jnp.int32, (BS, BS), 0) == lax.broadcasted_iota(jnp.int32, (BS, BS), 1)
    only = jnp.where(eye, full, 0.0)
    srow = lax.rsqrt(jnp.sum(only, axis=0, keepdims=True))
    srow_ref[...] = jnp.broadcast_to(srow, (8, BS))
    a_ref[:BS, :] = full * srow * lax.rsqrt(jnp.sum(only, axis=1, keepdims=True))
    lane = lax.broadcasted_iota(jnp.int32, (8, BS), 1)
    sub = lax.broadcasted_iota(jnp.int32, (8, BS), 0)
    for g in range(BS // GR):
        lo = g * GR
        ing = (lane >= lo) & (lane < lo + GR)
        p = a_ref[lo:lo + 8, :]
        cols = [jnp.broadcast_to(p[:, lo + j:lo + j + 1], (8, BS)) for j in range(GR)]
        x = jnp.where(lane == sub + lo, 1.0, jnp.where(ing, 0.0, p))
        w = x
        for j in range(0, GR, 2):
            cj, ck = cols[j], cols[j + 1]

            def row(v, i):
                return jnp.broadcast_to(v[i:i + 1, :], (8, BS))
            a, b, c = row(cj, j), row(cj, j + 1), row(ck, j + 1)
            det = a * c - b * b
            pair = (sub == j) | (sub == j + 1)
            cjm = jnp.where(sub == j, -1.0, jnp.where(sub == j + 1, 0.0, cj))
            ckm = jnp.where(sub == j + 1, -1.0, jnp.where(sub == j, 0.0, ck))
            r = recip(det)
            x0, x1 = row(x, j), row(x, j + 1)
            y1 = a * x1 - b * x0
            w = jnp.where(sub == j, x0 * lax.rsqrt(a), jnp.where(sub == j + 1, y1 * lax.rsqrt(a * det), w))
            for m in list(range(j + 2, GR)) + [-1]:
                v = x if m < 0 else cols[m]
                v0, v1 = row(v, j), row(v, j + 1)
                y0 = c * v0 - b * v1
                y1 = a * v1 - b * v0
                z = cjm * y0 + ckm * y1
                new = jnp.where(pair, 0.0, v) - r * z
                if m < 0:
                    x = new
                else:
                    cols[m] = new
        w_ref[lo:lo + 8, :] = jnp.where(lane < lo + GR, w, 0.0)
        for h in range(g + 1, BS // GR):
            q = a_ref[h * 8:h * 8 + 8, :]
            cs = [jnp.broadcast_to(q[:, lo + j:lo + j + 1], (8, BS)) for j in range(GR)]
            t = [cs[j] * jnp.broadcast_to(x[j:j + 1, :], (8, BS)) for j in range(GR)]
            while len(t) > 1:
                t = [t[i] + t[i + 1] for i in range(0, len(t), 2)]
            a_ref[h * 8:h * 8 + 8, :] = jnp.where(ing, 0.0, q) - t[0]


def device_of(q):
    return (q * 8) // 5


EARLY = ((0, 0), (1, 0), (1, 1))


def kernel(n_root, columns_ref, tiles_in, y0_in, o_ref, tiles_ref, y0_ref, wt, ys, hl, hr, gath, gb, ub, part, inbox,
           a_ref, w_ref, srow, whi, wlo, lhi, llo, r_ref, xhi, xlo,
           ls, hs, hrl, hrr, fs, fr, gs, gr, ds, dr, es, er, us, ur, uf, ub_sem):
    loads = [pltpu.make_async_copy(a, b, ls.at[n]) for n, (a, b) in enumerate(((y0_in, y0_ref), (tiles_in, tiles_ref)))]
    for load in loads:
        load.start()
    r, v = lax.axis_index("rows"), lax.axis_index("vecs")
    y, c = v // 2, v % 2
    sib, yr, yl = y * 2 + 1 - c, lax.rem(y + 1, NY) * 2 + c, lax.rem(y + NY - 1, NY) * 2 + c
    right, left = lax.rem(r + 1, NR), lax.rem(r + NR - 1, NR)

    barrier = pltpu.get_barrier_semaphore()

    def greet(d, _):
        pl.semaphore_signal(barrier, inc=1, device_id=(lax.rem(r + d, NR), v), device_id_type=MESH)
        return 0
    lax.fori_loop(1, NR, greet, 0)

    def greet_y(d, _):
        pl.semaphore_signal(barrier, inc=1, device_id=(r, lax.rem(y + d, NY) * 2 + c), device_id_type=MESH)
        return 0
    lax.fori_loop(1, NY, greet_y, 0)
    pl.semaphore_signal(barrier, inc=1, device_id=(r, sib), device_id_type=MESH)

    def rcopy(src, dst, send, recv, to):
        return pltpu.make_async_remote_copy(src_ref=src, dst_ref=dst, send_sem=send, recv_sem=recv, device_id=to, device_id_type=MESH)

    for load in loads:
        load.wait()
    wt[...] = jnp.zeros_like(wt)
    for b in range(4):
        rows = slice(b * BS, (b + 1) * BS)
        for t, o in ((0, 0), (1, -1), (2, 1)):
            wt[rows, (b + 3 + o) * BS:(b + 4 + o) * BS] = tiles_ref[b, t]
        for o in (-3, -2, 2, 3):
            want = lax.rem(r * 4 + b + o + 4 * NR, 4 * NR)
            tile = jnp.zeros((BS, BS), bf16)
            for t in (3, 4, 5):
                tile = jnp.where(columns_ref[b, t] == want, tiles_ref[b, t], tile)
            wt[rows, (b + 3 + o) * BS:(b + 4 + o) * BS] = tile

    pl.semaphore_wait(barrier, NR - 1 + NY - 1 + 1)

    def stacked(x):
        return jnp.concatenate(split(x), axis=0)

    def halves(x):
        n = x.shape[0] // 2
        return x[:n] + x[n:]

    waits = []
    rows_of = (slice(0, HALF), slice(HALF, 2 * HALF))

    def field(s):
        return y0_ref if s == 0 else ys.at[s - 1]

    def halo(s, h, go):
        src, n = field(s), 2 * s + h
        to_right = rcopy(src.at[rows_of[h], W - HALO:], hl.at[s, rows_of[h]], hs.at[2 * n], hrl.at[n], (right, v))
        to_left = rcopy(src.at[rows_of[h], :HALO], hr.at[s, rows_of[h]], hs.at[2 * n + 1], hrr.at[n], (left, v))
        if go:
            to_right.start()
            to_left.start()
            waits.extend((to_right, to_left))
        else:
            to_right.wait_recv()
            to_left.wait_recv()

    def ring(half, send, recv):
        started = set()

        def slot(d):
            return lax.rem(y + NY + d, NY) * 2 + c

        def other(d):
            return lax.rem(y + NY + d, NY) * 2 + 1 - c

        def go(i, n, h, to):
            rcopy(half(i, h), half(i, h), send.at[2 * n + h], recv.at[2 * n + h], (r, to)).start()
            started.add((n, h))

        def finish():
            for n, h in sorted(started):
                rcopy(half(v, h), half(v, h), send.at[2 * n + h], recv.at[2 * n + h], (r, sib)).wait_send()

        def arrive(i, n, h):
            rcopy(half(i, h), half(i, h), send.at[2 * n + h], recv.at[2 * n + h], (r, sib)).wait_recv()

        def first(h):
            go(v, 0, h, yr)
            go(v, 4, h, yl)
            go(v, 11, h, sib)

        def hop(s):
            for h in range(2):
                arrive(slot(-s), s - 1, h)
                if s < 3 or h == 0:
                    go(slot(-s), s, h, yr)
                go(slot(-s), 11 - s, h, sib)
                arrive(slot(s), 3 + s, h)
                if s < 3 or h == 1:
                    go(slot(s), 4 + s, h, yl)
                go(slot(s), 11 + s, h, sib)

        def across(d):
            for h in range(2):
                arrive(other(d), 15 if d == 4 else 11 + d, h)

        def last():
            arrive(slot(4), 3, 0)
            go(slot(4), 15, 0, sib)
            arrive(slot(4), 7, 1)
            go(slot(4), 15, 1, sib)
        return types.SimpleNamespace(first=first, hop=hop, across=across, last=last, finish=finish)

    vectors = ring(lambda i, h: gath.at[i, rows_of[h]], fs, fr)
    grams = ring(lambda i, h: gb.at[i, 10 * h:10 * h + 10], gs, gr)

    halo(0, 0, True)
    halo(0, 1, True)
    for s in range(4):
        acc = halves(mm(stacked(field(s)[...]), wt[:, HALO:HALO + W], True))
        for h in range(2):
            rows = rows_of[h]
            halo(s, h, False)
            wl = halves(mm(stacked(hl[s, rows]), wt[:HALO, :HALO], True))
            wr = halves(mm(stacked(hr[s, rows]), wt[BS:, HALO + W:], True))
            mid = acc[rows]
            parts = [mid[:, :BS] + wl[:, :BS], mid[:, BS:HALO] + wl[:, BS:] + wr[:, :2 * BS], mid[:, HALO:] + wr[:, 2 * BS:]]
            new = jnp.concatenate(parts, axis=1)
            if s:
                new = 2.0 * new - field(s - 1)[rows]
            if s < 3:
                ys[s, rows] = new
                halo(s + 1, h, True)
            else:
                gath[v, rows] = new
                vectors.first(h)

    own = split(gath[v])

    def gram_part(d):
        at = lax.rem(y + NY - d, NY)
        pair = split(gath[pl.ds(at * 2, 2)].reshape(BS, W))
        g = mm3(own, pair, True)
        for t in range(4):
            q = d * 4 + t
            part[q] = g[t * 16:(t + 1) * 16]
            to = device_of(q)
            rel = lax.rem(r - to + NR, NR)

            @pl.when(r != to)
            def _():
                rcopy(part.at[q], inbox.at[rel], ds.at[q], dr.at[rel], (to, v)).start()

    z = r % 8
    zq = (z * 5 + 4) // 8
    mine = (r // 8) * 5 + zq
    active = (zq * 8) // 5 == z

    def share(d):
        @pl.when(active & (mine // 4 == d))
        def _():
            def add(rel, total):
                rcopy(part.at[0], inbox.at[rel], ds.at[0], dr.at[rel], (right, v)).wait_recv()
                return total + inbox[rel]
            gb[v, mine] = lax.fori_loop(1, NR, add, part[mine])

            def send(rel, _):
                rcopy(gb.at[v, mine], gb.at[v, mine], es.at[rel], er.at[mine], (lax.rem(r + rel, NR), v)).start()
                return 0
            lax.fori_loop(1, NR, send, 0)

    def shared(d):
        for q in range(4 * d, 4 * d + 4):
            @pl.when(r != device_of(q))
            def _():
                rcopy(gb.at[v, q], gb.at[v, q], es.at[0], er.at[q], (right, v)).wait_recv()

    vectors.hop(1)
    vectors.across(0)
    gram_part(0)
    vectors.hop(2)
    vectors.across(-1)
    gram_part(1)
    vectors.hop(3)
    vectors.across(-2)
    gram_part(2)
    share(0)
    vectors.across(-3)
    gram_part(3)
    vectors.last()
    vectors.across(4)
    gram_part(4)
    for d in range(1, ND):
        share(d)
    shared(0)
    shared(1)

    def early(n):
        i, j = EARLY[n]
        d = i - j
        return i, gb.at[v, 4 * d:4 * d + 4], ub.at[n, c]

    for n in range(3):
        i, src, dst = early(n)

        @pl.when(y == i)
        def _():
            ub[n, c] = src[...]
            rcopy(src, dst, us.at[8 * n], ub_sem.at[n], (r, sib)).start()

            def one(m, _):
                rcopy(src, dst, us.at[8 * n + m], ur.at[n], (r, lax.rem(y + m, NY) * 2 + c)).start()
                return 0
            lax.fori_loop(1, NY, one, 0)
    for d in range(2, ND):
        shared(d)
    for h in range(2):
        grams.first(h)
    for n in range(3):
        i, src, dst = early(n)

        @pl.when(y != i)
        def _():
            rcopy(dst, dst, us.at[0], ur.at[n], (r, sib)).wait_recv()
            rcopy(dst, dst, uf.at[n], ub_sem.at[n], (r, sib)).start()
    for n in range(3):
        dst = ub.at[n, 1 - c]
        rcopy(dst, dst, us.at[0], ub_sem.at[n], (r, sib)).wait_recv()

    def block(i, j):
        d = i - j
        if d <= 4:
            return gb[2 * i:2 * i + 2, 4 * d:4 * d + 4].reshape(BS, BS)
        d = NB - d
        return gb[2 * j:2 * j + 2, 4 * d:4 * d + 4].reshape(BS, BS).T

    def column(k, first=0):
        top = (k + first) * BS
        s = jnp.concatenate([block(i, k) for i in range(k + first, NB)], axis=0)
        if k:
            rows = (lhi[top:, :k * BS], llo[top:, :k * BS])
            own = (lhi[k * BS:(k + 1) * BS, :k * BS], llo[k * BS:(k + 1) * BS, :k * BS])
            s = s - mm3(rows, own, True)
        return s

    def panel(k, first, rows):
        h, l = split(mm3(split(rows), (whi[k], wlo[k]), True))
        stop = first * BS + rows.shape[0]
        lhi[first * BS:stop, k * BS:(k + 1) * BS] = h
        llo[first * BS:stop, k * BS:(k + 1) * BS] = l
        return h, l

    def after(k):
        whi[k], wlo[k] = split(w_ref[...] * srow[0:1, :])
        if k == 0:
            low = panel(0, 1, ub[1].reshape(BS, BS))
            a_ref[:BS, :] = ub[2].reshape(BS, BS) - mm3(low, low, True)
            grams.hop(2)
        elif k == 1:
            grams.hop(3)
            for d in (0, -1, -2, -3, 1, 2, 3):
                grams.across(d)
            grams.last()
            grams.across(4)
            panel(0, 2, column(0, 2))
            panel(1, 2, column(1, 1))
            a_ref[0:M - 2 * BS, :] = column(2)
        elif k + 1 < NB:
            panel(k, k + 1, a_ref[BS:M - k * BS, :])
            a_ref[0:M - (k + 1) * BS, :] = column(k + 1)

    def step(k, _):
        diag_factor(a_ref, w_ref, srow)
        for kk in range(NB):
            @pl.when(k == kk)
            def _():
                after(kk)
        return 0
    a_ref[:BS, :] = ub[0].reshape(BS, BS)
    grams.hop(1)
    lax.fori_loop(0, NB, step, 0)

    sel = lax.broadcasted_iota(jnp.int32, (64, M), 0) + v * 64 == lax.broadcasted_iota(jnp.int32, (64, M), 1)
    r_ref[...] = jnp.where(sel, f32(n_root), 0.0)
    for k in range(NB - 1, -1, -1):
        x = split(mm3(split(r_ref[:, k * BS:(k + 1) * BS]), (whi[k], wlo[k])))
        if k:
            r_ref[:, :k * BS] -= mm3(x, (lhi[k * BS:(k + 1) * BS, :k * BS], llo[k * BS:(k + 1) * BS, :k * BS]))
        xhi[:, k * BS:(k + 1) * BS] = x[0]
        xlo[:, k * BS:(k + 1) * BS] = x[1]
    for d in (1, 2, 3):
        vectors.across(d)
    o_ref[...] = mm3((xhi[...], xlo[...]), split(gath[...].reshape(M, W)))

    for k in waits:
        k.wait_send()
    vectors.finish()
    grams.finish()
    for q in range(NQ):
        @pl.when(r != device_of(q))
        def _():
            rcopy(part.at[q], inbox.at[0], ds.at[q], dr.at[0], (right, v)).wait_send()

    @pl.when(active)
    def _():
        def done(rel, _):
            rcopy(gb.at[v, mine], gb.at[v, mine], es.at[rel], er.at[mine], (right, v)).wait_send()
            return 0
        lax.fori_loop(1, NR, done, 0)

    for n in range(3):
        i, src, dst = early(n)

        @pl.when(y == i)
        def _():
            def sent(m, _):
                rcopy(src, dst, us.at[8 * n + m], ur.at[n], (r, sib)).wait_send()
                return 0
            lax.fori_loop(0, NY, sent, 0)

        @pl.when(y != i)
        def _():
            rcopy(dst, dst, uf.at[n], ub_sem.at[n], (r, sib)).wait_send()


def solve(tiles, columns, start, n_root=128.0):
    vm = pl.BlockSpec(memory_space=pltpu.VMEM)
    dma = pltpu.SemaphoreType.DMA
    return pl.pallas_call(
        functools.partial(kernel, n_root),
        out_shape=jax.ShapeDtypeStruct((64, W), f32),
        in_specs=[pl.BlockSpec(memory_space=pltpu.SMEM), pl.BlockSpec(memory_space=pl.ANY), pl.BlockSpec(memory_space=pl.ANY)],
        out_specs=vm,
        scratch_shapes=[
            pltpu.VMEM((4, 6, BS, BS), bf16), pltpu.VMEM((64, W), f32),
            pltpu.VMEM((W, W + 2 * HALO), bf16), pltpu.VMEM((3, 64, W), f32),
            pltpu.VMEM((4, 64, HALO), f32), pltpu.VMEM((4, 64, HALO), f32),
            pltpu.VMEM((16, 64, W), f32), pltpu.VMEM((16, NQ, 16, BS), f32),
            pltpu.VMEM((3, 2, 4, 16, BS), f32),
            pltpu.VMEM((NQ, 16, BS), f32), pltpu.VMEM((NR, 16, BS), f32),
            pltpu.VMEM((M, BS), f32), pltpu.VMEM((BS, BS), f32), pltpu.VMEM((8, BS), f32),
            pltpu.VMEM((NB, BS, BS), bf16), pltpu.VMEM((NB, BS, BS), bf16),
            pltpu.VMEM((M, M), bf16), pltpu.VMEM((M, M), bf16),
            pltpu.VMEM((64, M), f32), pltpu.VMEM((64, M), bf16), pltpu.VMEM((64, M), bf16),
            dma((2,)), dma((16,)), dma((8,)), dma((8,)), dma((32,)), dma((32,)), dma((32,)), dma((32,)),
            dma((NQ,)), dma((NR,)), dma((NR,)), dma((NQ,)),
            dma((24,)), dma((3,)), dma((3,)), dma((3,))],
        compiler_params=pltpu.CompilerParams(collective_id=0, has_side_effects=True, vmem_limit_bytes=56 << 20),
    )(columns, tiles, start)


def solution(mesh):
    placed = (P("rows", None, None, None), P("rows", None), P("vecs", "rows"))
    return jax.shard_map(
        solve, mesh=mesh, in_specs=placed, out_specs=P("vecs", "rows"), check_vma=False
    )
```

```python
import functools
import types

import jax
import jax.numpy as jnp
from jax import lax
from jax.experimental import pallas as pl
from jax.experimental.pallas import tpu as pltpu
from jax.sharding import PartitionSpec as P

f32, bf16 = jnp.float32, jnp.bfloat16
M, BS, NB, GR = 1024, 128, 8, 8
MESH = pl.DeviceIdType.MESH
NR, NY, ND, NQ = 32, 8, 5, 20
HALO, W, HALF = 384, 512, 32


def split(x):
    hi = x.astype(bf16)
    return hi, (x - hi.astype(f32)).astype(bf16)


def mm(a, b, tb):
    dims = (((1,), (1 if tb else 0,)), ((), ()))
    return lax.dot_general(a, b, dims, preferred_element_type=f32)


def mm3(a, b, tb=False):
    return mm(a[0], b[0], tb) + (mm(a[0], b[1], tb) + mm(a[1], b[0], tb))


def recip(x):
    r = pl.reciprocal(x, approx=True)
    return r * (2.0 - x * r)


def diag_factor(a_ref, w_ref, srow_ref):
    full = a_ref[:BS, :]
    eye = lax.broadcasted_iota(jnp.int32, (BS, BS), 0) == lax.broadcasted_iota(jnp.int32, (BS, BS), 1)
    only = jnp.where(eye, full, 0.0)
    srow = lax.rsqrt(jnp.sum(only, axis=0, keepdims=True))
    srow_ref[...] = jnp.broadcast_to(srow, (8, BS))
    a_ref[:BS, :] = full * srow * lax.rsqrt(jnp.sum(only, axis=1, keepdims=True))
    lane = lax.broadcasted_iota(jnp.int32, (8, BS), 1)
    sub = lax.broadcasted_iota(jnp.int32, (8, BS), 0)
    for g in range(BS // GR):
        lo = g * GR
        ing = (lane >= lo) & (lane < lo + GR)
        p = a_ref[lo:lo + 8, :]
        cols = [jnp.broadcast_to(p[:, lo + j:lo + j + 1], (8, BS)) for j in range(GR)]
        x = jnp.where(lane == sub + lo, 1.0, jnp.where(ing, 0.0, p))
        w = x
        for j in range(0, GR, 2):
            cj, ck = cols[j], cols[j + 1]

            def row(v, i):
                return jnp.broadcast_to(v[i:i + 1, :], (8, BS))
            a, b, c = row(cj, j), row(cj, j + 1), row(ck, j + 1)
            det = a * c - b * b
            pair = (sub == j) | (sub == j + 1)
            cjm = jnp.where(sub == j, -1.0, jnp.where(sub == j + 1, 0.0, cj))
            ckm = jnp.where(sub == j + 1, -1.0, jnp.where(sub == j, 0.0, ck))
            r = recip(det)
            x0, x1 = row(x, j), row(x, j + 1)
            y1 = a * x1 - b * x0
            w = jnp.where(sub == j, x0 * lax.rsqrt(a), jnp.where(sub == j + 1, y1 * lax.rsqrt(a * det), w))
            for m in list(range(j + 2, GR)) + [-1]:
                v = x if m < 0 else cols[m]
                v0, v1 = row(v, j), row(v, j + 1)
                y0 = c * v0 - b * v1
                y1 = a * v1 - b * v0
                z = cjm * y0 + ckm * y1
                new = jnp.where(pair, 0.0, v) - r * z
                if m < 0:
                    x = new
                else:
                    cols[m] = new
        w_ref[lo:lo + 8, :] = jnp.where(lane < lo + GR, w, 0.0)
        for h in range(g + 1, BS // GR):
            q = a_ref[h * 8:h * 8 + 8, :]
            cs = [jnp.broadcast_to(q[:, lo + j:lo + j + 1], (8, BS)) for j in range(GR)]
            t = [cs[j] * jnp.broadcast_to(x[j:j + 1, :], (8, BS)) for j in range(GR)]
            while len(t) > 1:
                t = [t[i] + t[i + 1] for i in range(0, len(t), 2)]
            a_ref[h * 8:h * 8 + 8, :] = jnp.where(ing, 0.0, q) - t[0]


def device_of(q):
    return (q * 8) // 5


EARLY = 3


def kernel(n_root, columns_ref, tiles_in, y0_in, o_ref, tiles_ref, y0_ref, wt, ys, hl, hr, gath, gb, ub0, ub1, ub2, part, inbox,
           a_ref, w_ref, srow, whi, wlo, lhi, llo, r_ref, xhi, xlo,
           ls, hs, hrl, hrr, fs, fr, gs, gr, ds, dr, es, er, us, ur, uf, ub_sem):
    loads = [pltpu.make_async_copy(a, b, ls.at[n]) for n, (a, b) in enumerate(((y0_in, y0_ref), (tiles_in, tiles_ref)))]
    for load in loads:
        load.start()
    r, v = lax.axis_index("rows"), lax.axis_index("vecs")
    y, c = v // 2, v % 2
    sib, yr, yl = y * 2 + 1 - c, lax.rem(y + 1, NY) * 2 + c, lax.rem(y + NY - 1, NY) * 2 + c
    right, left = lax.rem(r + 1, NR), lax.rem(r + NR - 1, NR)

    barrier = pltpu.get_barrier_semaphore()

    def greet(d, _):
        pl.semaphore_signal(barrier, inc=1, device_id=(lax.rem(r + d, NR), v), device_id_type=MESH)
        return 0
    lax.fori_loop(1, NR, greet, 0)

    def greet_y(d, _):
        pl.semaphore_signal(barrier, inc=1, device_id=(r, lax.rem(y + d, NY) * 2 + c), device_id_type=MESH)
        return 0
    lax.fori_loop(1, NY, greet_y, 0)
    pl.semaphore_signal(barrier, inc=1, device_id=(r, sib), device_id_type=MESH)

    def rcopy(src, dst, send, recv, to):
        return pltpu.make_async_remote_copy(src_ref=src, dst_ref=dst, send_sem=send, recv_sem=recv, device_id=to, device_id_type=MESH)

    for load in loads:
        load.wait()
    wt[...] = jnp.zeros_like(wt)
    for b in range(4):
        rows = slice(b * BS, (b + 1) * BS)
        for t, o in ((0, 0), (1, -1), (2, 1)):
            wt[rows, (b + 3 + o) * BS:(b + 4 + o) * BS] = tiles_ref[b, t]
        for o in (-3, -2, 2, 3):
            want = lax.rem(r * 4 + b + o + 4 * NR, 4 * NR)
            tile = jnp.zeros((BS, BS), bf16)
            for t in (3, 4, 5):
                tile = jnp.where(columns_ref[b, t] == want, tiles_ref[b, t], tile)
            wt[rows, (b + 3 + o) * BS:(b + 4 + o) * BS] = tile

    pl.semaphore_wait(barrier, NR - 1 + NY - 1 + 1)

    def stacked(x):
        return jnp.concatenate(split(x), axis=0)

    def halves(x):
        n = x.shape[0] // 2
        return x[:n] + x[n:]

    waits = []
    rows_of = (slice(0, HALF), slice(HALF, 2 * HALF))

    def field(s):
        return y0_ref if s == 0 else ys.at[s - 1]

    def halo(s, h, go):
        src, n = field(s), 2 * s + h
        to_right = rcopy(src.at[rows_of[h], W - HALO:], hl.at[s, rows_of[h]], hs.at[2 * n], hrl.at[n], (right, v))
        to_left = rcopy(src.at[rows_of[h], :HALO], hr.at[s, rows_of[h]], hs.at[2 * n + 1], hrr.at[n], (left, v))
        if go:
            to_right.start()
            to_left.start()
            waits.extend((to_right, to_left))
        else:
            to_right.wait_recv()
            to_left.wait_recv()

    def ring(half, send, recv):
        started = set()

        def slot(d):
            return lax.rem(y + NY + d, NY) * 2 + c

        def other(d):
            return lax.rem(y + NY + d, NY) * 2 + 1 - c

        def go(i, n, h, to):
            rcopy(half(i, h), half(i, h), send.at[2 * n + h], recv.at[2 * n + h], (r, to)).start()
            started.add((n, h))

        def finish():
            for n, h in sorted(started):
                rcopy(half(v, h), half(v, h), send.at[2 * n + h], recv.at[2 * n + h], (r, sib)).wait_send()

        def arrive(i, n, h):
            rcopy(half(i, h), half(i, h), send.at[2 * n + h], recv.at[2 * n + h], (r, sib)).wait_recv()

        def first(h):
            go(v, 0, h, yr)
            go(v, 4, h, yl)
            go(v, 11, h, sib)

        def hop(s):
            for h in range(2):
                arrive(slot(-s), s - 1, h)
                if s < 3 or h == 0:
                    go(slot(-s), s, h, yr)
                go(slot(-s), 11 - s, h, sib)
                arrive(slot(s), 3 + s, h)
                if s < 3 or h == 1:
                    go(slot(s), 4 + s, h, yl)
                go(slot(s), 11 + s, h, sib)

        def across(d):
            for h in range(2):
                arrive(other(d), 15 if d == 4 else 11 + d, h)

        def last():
            arrive(slot(4), 3, 0)
            go(slot(4), 15, 0, sib)
            arrive(slot(4), 7, 1)
            go(slot(4), 15, 1, sib)
        return types.SimpleNamespace(first=first, hop=hop, across=across, last=last, finish=finish)

    vectors = ring(lambda i, h: gath.at[i, rows_of[h]], fs, fr)
    grams = ring(lambda i, h: gb.at[i, 10 * h:10 * h + 10], gs, gr)

    halo(0, 0, True)
    halo(0, 1, True)
    for s in range(4):
        acc = halves(mm(stacked(field(s)[...]), wt[:, HALO:HALO + W], True))
        for h in range(2):
            rows = rows_of[h]
            halo(s, h, False)
            wl = halves(mm(stacked(hl[s, rows]), wt[:HALO, :HALO], True))
            wr = halves(mm(stacked(hr[s, rows]), wt[BS:, HALO + W:], True))
            mid = acc[rows]
            parts = [mid[:, :BS] + wl[:, :BS], mid[:, BS:HALO] + wl[:, BS:] + wr[:, :2 * BS], mid[:, HALO:] + wr[:, 2 * BS:]]
            new = jnp.concatenate(parts, axis=1)
            if s:
                new = 2.0 * new - field(s - 1)[rows]
            if s < 3:
                ys[s, rows] = new
                halo(s + 1, h, True)
            else:
                gath[v, rows] = new
                vectors.first(h)

    own = split(gath[v])

    def gram_part(d):
        at = lax.rem(y + NY - d, NY)
        pair = split(gath[pl.ds(at * 2, 2)].reshape(BS, W))
        g = mm3(own, pair, True)
        for t in range(4):
            q = d * 4 + t
            part[q] = g[t * 16:(t + 1) * 16]
            to = device_of(q)
            rel = lax.rem(r - to + NR, NR)

            @pl.when(r != to)
            def _():
                rcopy(part.at[q], inbox.at[rel], ds.at[q], dr.at[rel], (to, v)).start()

    z = r % 8
    zq = (z * 5 + 4) // 8
    mine = (r // 8) * 5 + zq
    active = (zq * 8) // 5 == z

    def share(d):
        @pl.when(active & (mine // 4 == d))
        def _():
            def add(rel, total):
                rcopy(part.at[0], inbox.at[rel], ds.at[0], dr.at[rel], (right, v)).wait_recv()
                return total + inbox[rel]
            gb[v, mine] = lax.fori_loop(1, NR, add, part[mine])

            def send(rel, _):
                rcopy(gb.at[v, mine], gb.at[v, mine], es.at[rel], er.at[mine], (lax.rem(r + rel, NR), v)).start()
                return 0
            lax.fori_loop(1, NR, send, 0)

    def shared(d):
        for q in range(4 * d, 4 * d + 4):
            @pl.when(r != device_of(q))
            def _():
                rcopy(gb.at[v, q], gb.at[v, q], es.at[0], er.at[q], (right, v)).wait_recv()

    vectors.hop(1)
    vectors.across(0)
    gram_part(0)
    vectors.hop(2)
    vectors.across(-1)
    gram_part(1)
    vectors.hop(3)
    vectors.across(-2)
    gram_part(2)
    share(0)
    vectors.across(-3)
    gram_part(3)
    share(1)
    vectors.last()
    vectors.across(4)
    gram_part(4)

    ub = (ub0, ub1, ub2)

    def early(i, core):
        return gb.at[v, :4 * i + 4], ub[i].at[core]

    def send_early(i):
        src, dst = early(i, c)

        @pl.when(y == i)
        def _():
            dst[...] = src[...]
            rcopy(src, dst, us.at[8 * i], ub_sem.at[i], (r, sib)).start()

            def one(m, _):
                rcopy(src, dst, us.at[8 * i + m], ur.at[i], (r, lax.rem(y + m, NY) * 2 + c)).start()
                return 0
            lax.fori_loop(1, NY, one, 0)

    def pass_early(i):
        dst = early(i, c)[1]

        @pl.when(y != i)
        def _():
            rcopy(dst, dst, us.at[0], ur.at[i], (r, sib)).wait_recv()
            rcopy(dst, dst, uf.at[i], ub_sem.at[i], (r, sib)).start()

    def take_early(i):
        dst = early(i, 1 - c)[1]
        rcopy(dst, dst, us.at[0], ub_sem.at[i], (r, sib)).wait_recv()

    shared(0)
    send_early(0)
    shared(1)
    send_early(1)
    for d in range(2, ND):
        share(d)
    shared(2)
    send_early(2)
    pass_early(0)
    pass_early(1)
    shared(3)
    shared(4)
    for h in range(2):
        grams.first(h)
    take_early(0)
    take_early(1)

    def ahead(i, j):
        return ub[i][:, 4 * (i - j):4 * (i - j) + 4].reshape(BS, BS)

    def block(i, j):
        d = i - j
        if d <= 4:
            return gb[2 * i:2 * i + 2, 4 * d:4 * d + 4].reshape(BS, BS)
        d = NB - d
        return gb[2 * j:2 * j + 2, 4 * d:4 * d + 4].reshape(BS, BS).T

    def column(k, first=0):
        top = (k + first) * BS
        s = jnp.concatenate([block(i, k) for i in range(k + first, NB)], axis=0)
        if k:
            rows = (lhi[top:, :k * BS], llo[top:, :k * BS])
            own = (lhi[k * BS:(k + 1) * BS, :k * BS], llo[k * BS:(k + 1) * BS, :k * BS])
            s = s - mm3(rows, own, True)
        return s

    def panel(k, first, rows):
        h, l = split(mm3(split(rows), (whi[k], wlo[k]), True))
        stop = first * BS + rows.shape[0]
        lhi[first * BS:stop, k * BS:(k + 1) * BS] = h
        llo[first * BS:stop, k * BS:(k + 1) * BS] = l
        return h, l

    def after(k):
        whi[k], wlo[k] = split(w_ref[...] * srow[0:1, :])
        if k == 0:
            grams.hop(1)
            low = panel(0, 1, ahead(1, 0))
            a_ref[:BS, :] = ahead(1, 1) - mm3(low, low, True)
            pass_early(2)
        elif k == 1:
            take_early(2)
            grams.hop(2)
            low = panel(0, 2, ahead(2, 0))
            above = (lhi[BS:2 * BS, :BS], llo[BS:2 * BS, :BS])
            next_low = panel(1, 2, ahead(2, 1) - mm3(low, above, True))
            a_ref[:BS, :] = ahead(2, 2) - mm3(low, low, True) - mm3(next_low, next_low, True)
        elif k == 2:
            grams.hop(3)
            for d in (0, -1, -2, -3, 1, 2, 3):
                grams.across(d)
            grams.last()
            grams.across(4)
            for j in range(EARLY):
                panel(j, EARLY, column(j, EARLY - j))
            a_ref[0:M - EARLY * BS, :] = column(EARLY)
        elif k + 1 < NB:
            panel(k, k + 1, a_ref[BS:M - k * BS, :])
            a_ref[0:M - (k + 1) * BS, :] = column(k + 1)

    def step(k, _):
        diag_factor(a_ref, w_ref, srow)
        for kk in range(NB):
            @pl.when(k == kk)
            def _():
                after(kk)
        return 0
    a_ref[:BS, :] = ahead(0, 0)
    lax.fori_loop(0, NB, step, 0)

    sel = lax.broadcasted_iota(jnp.int32, (64, M), 0) + v * 64 == lax.broadcasted_iota(jnp.int32, (64, M), 1)
    r_ref[...] = jnp.where(sel, f32(n_root), 0.0)
    for k in range(NB - 1, -1, -1):
        x = split(mm3(split(r_ref[:, k * BS:(k + 1) * BS]), (whi[k], wlo[k])))
        if k:
            r_ref[:, :k * BS] -= mm3(x, (lhi[k * BS:(k + 1) * BS, :k * BS], llo[k * BS:(k + 1) * BS, :k * BS]))
        xhi[:, k * BS:(k + 1) * BS] = x[0]
        xlo[:, k * BS:(k + 1) * BS] = x[1]
    for d in (1, 2, 3):
        vectors.across(d)
    o_ref[...] = mm3((xhi[...], xlo[...]), split(gath[...].reshape(M, W)))

    for k in waits:
        k.wait_send()
    vectors.finish()
    grams.finish()
    for q in range(NQ):
        @pl.when(r != device_of(q))
        def _():
            rcopy(part.at[q], inbox.at[0], ds.at[q], dr.at[0], (right, v)).wait_send()

    @pl.when(active)
    def _():
        def done(rel, _):
            rcopy(gb.at[v, mine], gb.at[v, mine], es.at[rel], er.at[mine], (right, v)).wait_send()
            return 0
        lax.fori_loop(1, NR, done, 0)

    for i in range(EARLY):
        src, dst = early(i, c)

        @pl.when(y == i)
        def _():
            def sent(m, _):
                rcopy(src, dst, us.at[8 * i + m], ur.at[i], (r, sib)).wait_send()
                return 0
            lax.fori_loop(0, NY, sent, 0)

        @pl.when(y != i)
        def _():
            rcopy(dst, dst, uf.at[i], ub_sem.at[i], (r, sib)).wait_send()


def solve(tiles, columns, start, n_root=128.0):
    vm = pl.BlockSpec(memory_space=pltpu.VMEM)
    dma = pltpu.SemaphoreType.DMA
    return pl.pallas_call(
        functools.partial(kernel, n_root),
        out_shape=jax.ShapeDtypeStruct((64, W), f32),
        in_specs=[pl.BlockSpec(memory_space=pltpu.SMEM), pl.BlockSpec(memory_space=pl.ANY), pl.BlockSpec(memory_space=pl.ANY)],
        out_specs=vm,
        scratch_shapes=[
            pltpu.VMEM((4, 6, BS, BS), bf16), pltpu.VMEM((64, W), f32),
            pltpu.VMEM((W, W + 2 * HALO), bf16), pltpu.VMEM((3, 64, W), f32),
            pltpu.VMEM((4, 64, HALO), f32), pltpu.VMEM((4, 64, HALO), f32),
            pltpu.VMEM((16, 64, W), f32), pltpu.VMEM((16, NQ, 16, BS), f32),
            pltpu.VMEM((2, 4, 16, BS), f32), pltpu.VMEM((2, 8, 16, BS), f32), pltpu.VMEM((2, 12, 16, BS), f32),
            pltpu.VMEM((NQ, 16, BS), f32), pltpu.VMEM((NR, 16, BS), f32),
            pltpu.VMEM((M, BS), f32), pltpu.VMEM((BS, BS), f32), pltpu.VMEM((8, BS), f32),
            pltpu.VMEM((NB, BS, BS), bf16), pltpu.VMEM((NB, BS, BS), bf16),
            pltpu.VMEM((M, M), bf16), pltpu.VMEM((M, M), bf16),
            pltpu.VMEM((64, M), f32), pltpu.VMEM((64, M), bf16), pltpu.VMEM((64, M), bf16),
            dma((2,)), dma((16,)), dma((8,)), dma((8,)), dma((32,)), dma((32,)), dma((32,)), dma((32,)),
            dma((NQ,)), dma((NR,)), dma((NR,)), dma((NQ,)),
            dma((24,)), dma((3,)), dma((3,)), dma((3,))],
        compiler_params=pltpu.CompilerParams(collective_id=0, has_side_effects=True, vmem_limit_bytes=56 << 20),
    )(columns, tiles, start)


def solution(mesh):
    placed = (P("rows", None, None, None), P("rows", None), P("vecs", "rows"))
    return jax.shard_map(
        solve, mesh=mesh, in_specs=placed, out_specs=P("vecs", "rows"), check_vma=False
    )
```

```python
import functools
import types

import jax
import jax.numpy as jnp
from jax import lax
from jax.experimental import pallas as pl
from jax.experimental.pallas import tpu as pltpu
from jax.sharding import PartitionSpec as P

f32, bf16 = jnp.float32, jnp.bfloat16
M, BS, NB, GR = 1024, 128, 8, 8
MESH = pl.DeviceIdType.MESH
NR, NY, ND, NQ = 32, 8, 5, 20
HALO, W, HALF = 384, 512, 32


def split(x):
    hi = x.astype(bf16)
    return hi, (x - hi.astype(f32)).astype(bf16)


def mm(a, b, tb):
    dims = (((1,), (1 if tb else 0,)), ((), ()))
    return lax.dot_general(a, b, dims, preferred_element_type=f32)


def mm3(a, b, tb=False):
    return mm(a[0], b[0], tb) + (mm(a[0], b[1], tb) + mm(a[1], b[0], tb))


def recip(x):
    r = pl.reciprocal(x, approx=True)
    return r * (2.0 - x * r)


def diag_factor(a_ref, w_ref, srow_ref):
    full = a_ref[:BS, :]
    eye = lax.broadcasted_iota(jnp.int32, (BS, BS), 0) == lax.broadcasted_iota(jnp.int32, (BS, BS), 1)
    only = jnp.where(eye, full, 0.0)
    srow = lax.rsqrt(jnp.sum(only, axis=0, keepdims=True))
    srow_ref[...] = jnp.broadcast_to(srow, (8, BS))
    a_ref[:BS, :] = full * srow * lax.rsqrt(jnp.sum(only, axis=1, keepdims=True))
    lane = lax.broadcasted_iota(jnp.int32, (8, BS), 1)
    sub = lax.broadcasted_iota(jnp.int32, (8, BS), 0)
    for g in range(BS // GR):
        lo = g * GR
        ing = (lane >= lo) & (lane < lo + GR)
        p = a_ref[lo:lo + 8, :]
        cols = [jnp.broadcast_to(p[:, lo + j:lo + j + 1], (8, BS)) for j in range(GR)]
        x = jnp.where(lane == sub + lo, 1.0, jnp.where(ing, 0.0, p))
        w = x
        for j in range(0, GR, 2):
            cj, ck = cols[j], cols[j + 1]

            def row(v, i):
                return jnp.broadcast_to(v[i:i + 1, :], (8, BS))
            a, b, c = row(cj, j), row(cj, j + 1), row(ck, j + 1)
            det = a * c - b * b
            pair = (sub == j) | (sub == j + 1)
            cjm = jnp.where(sub == j, -1.0, jnp.where(sub == j + 1, 0.0, cj))
            ckm = jnp.where(sub == j + 1, -1.0, jnp.where(sub == j, 0.0, ck))
            r = recip(det)
            x0, x1 = row(x, j), row(x, j + 1)
            y1 = a * x1 - b * x0
            w = jnp.where(sub == j, x0 * lax.rsqrt(a), jnp.where(sub == j + 1, y1 * lax.rsqrt(a * det), w))
            for m in list(range(j + 2, GR)) + [-1]:
                v = x if m < 0 else cols[m]
                v0, v1 = row(v, j), row(v, j + 1)
                y0 = c * v0 - b * v1
                y1 = a * v1 - b * v0
                z = cjm * y0 + ckm * y1
                new = jnp.where(pair, 0.0, v) - r * z
                if m < 0:
                    x = new
                else:
                    cols[m] = new
        w_ref[lo:lo + 8, :] = jnp.where(lane < lo + GR, w, 0.0)
        for h in range(g + 1, BS // GR):
            q = a_ref[h * 8:h * 8 + 8, :]
            cs = [jnp.broadcast_to(q[:, lo + j:lo + j + 1], (8, BS)) for j in range(GR)]
            t = [cs[j] * jnp.broadcast_to(x[j:j + 1, :], (8, BS)) for j in range(GR)]
            while len(t) > 1:
                t = [t[i] + t[i + 1] for i in range(0, len(t), 2)]
            a_ref[h * 8:h * 8 + 8, :] = jnp.where(ing, 0.0, q) - t[0]


def device_of(q):
    return (q * 8) // 5


EARLY = 3


def kernel(n_root, columns_ref, tiles_in, y0_in, o_ref, tiles_ref, y0_ref, wt, ys, hl, hr, gath, gb, ub0, ub1, ub2, part, inbox,
           a_ref, w_ref, srow, whi, wlo, lhi, llo, r_ref, xhi, xlo,
           ls, hs, hrl, hrr, fs, fr, gs, gr, ds, dr, es, er, us, ur, uf, ub_sem):
    loads = [pltpu.make_async_copy(a, b, ls.at[n]) for n, (a, b) in enumerate(((y0_in, y0_ref), (tiles_in, tiles_ref)))]
    for load in loads:
        load.start()
    r, v = lax.axis_index("rows"), lax.axis_index("vecs")
    y, c = v // 2, v % 2
    sib, yr, yl = y * 2 + 1 - c, lax.rem(y + 1, NY) * 2 + c, lax.rem(y + NY - 1, NY) * 2 + c
    right, left = lax.rem(r + 1, NR), lax.rem(r + NR - 1, NR)

    barrier = pltpu.get_barrier_semaphore()

    def greet(d, _):
        pl.semaphore_signal(barrier, inc=1, device_id=(lax.rem(r + d, NR), v), device_id_type=MESH)
        return 0
    lax.fori_loop(1, NR, greet, 0)

    def greet_y(d, _):
        pl.semaphore_signal(barrier, inc=1, device_id=(r, lax.rem(y + d, NY) * 2 + c), device_id_type=MESH)
        return 0
    lax.fori_loop(1, NY, greet_y, 0)
    pl.semaphore_signal(barrier, inc=1, device_id=(r, sib), device_id_type=MESH)

    def rcopy(src, dst, send, recv, to):
        return pltpu.make_async_remote_copy(src_ref=src, dst_ref=dst, send_sem=send, recv_sem=recv, device_id=to, device_id_type=MESH)

    for load in loads:
        load.wait()
    wt[...] = jnp.zeros_like(wt)
    for b in range(4):
        rows = slice(b * BS, (b + 1) * BS)
        for t, o in ((0, 0), (1, -1), (2, 1)):
            wt[rows, (b + 3 + o) * BS:(b + 4 + o) * BS] = tiles_ref[b, t]
        for o in (-3, -2, 2, 3):
            want = lax.rem(r * 4 + b + o + 4 * NR, 4 * NR)
            tile = jnp.zeros((BS, BS), bf16)
            for t in (3, 4, 5):
                tile = jnp.where(columns_ref[b, t] == want, tiles_ref[b, t], tile)
            wt[rows, (b + 3 + o) * BS:(b + 4 + o) * BS] = tile

    pl.semaphore_wait(barrier, NR - 1 + NY - 1 + 1)

    def stacked(x):
        return jnp.concatenate(split(x), axis=0)

    def halves(x):
        n = x.shape[0] // 2
        return x[:n] + x[n:]

    waits = []
    rows_of = (slice(0, HALF), slice(HALF, 2 * HALF))

    def field(s):
        return y0_ref if s == 0 else ys.at[s - 1]

    def halo(s, h, go):
        src, n = field(s), 2 * s + h
        to_right = rcopy(src.at[rows_of[h], W - HALO:], hl.at[s, rows_of[h]], hs.at[2 * n], hrl.at[n], (right, v))
        to_left = rcopy(src.at[rows_of[h], :HALO], hr.at[s, rows_of[h]], hs.at[2 * n + 1], hrr.at[n], (left, v))
        if go:
            to_right.start()
            to_left.start()
            waits.extend((to_right, to_left))
        else:
            to_right.wait_recv()
            to_left.wait_recv()

    def ring(half, send, recv):
        started = set()

        def slot(d):
            return lax.rem(y + NY + d, NY) * 2 + c

        def other(d):
            return lax.rem(y + NY + d, NY) * 2 + 1 - c

        def each(i, h, act):
            for when, ref in half(i, h):
                if when is None:
                    act(ref)
                else:
                    @pl.when(when)
                    def _():
                        act(ref)

        def go(i, n, h, to):
            each(i, h, lambda ref: rcopy(ref, ref, send.at[2 * n + h], recv.at[2 * n + h], (r, to)).start())
            started.add((n, h))

        def arrive(i, n, h):
            each(i, h, lambda ref: rcopy(ref, ref, send.at[2 * n + h], recv.at[2 * n + h], (r, sib)).wait_recv())

        def origin(n):
            if n < 4:
                return slot(-n)
            if n < 8:
                return slot(n - 4)
            return slot(n - 11) if n < 15 else slot(4)

        def finish():
            for n, h in sorted(started):
                each(origin(n), h, lambda ref: rcopy(ref, ref, send.at[2 * n + h], recv.at[2 * n + h], (r, sib)).wait_send())

        def first(h):
            go(v, 0, h, yr)
            go(v, 4, h, yl)
            go(v, 11, h, sib)

        def hop(s):
            for h in range(2):
                arrive(slot(-s), s - 1, h)
                if s < 3 or h == 0:
                    go(slot(-s), s, h, yr)
                go(slot(-s), 11 - s, h, sib)
                arrive(slot(s), 3 + s, h)
                if s < 3 or h == 1:
                    go(slot(s), 4 + s, h, yl)
                go(slot(s), 11 + s, h, sib)

        def across(d):
            for h in range(2):
                arrive(other(d), 15 if d == 4 else 11 + d, h)

        def last():
            arrive(slot(4), 3, 0)
            go(slot(4), 15, 0, sib)
            arrive(slot(4), 7, 1)
            go(slot(4), 15, 1, sib)
        return types.SimpleNamespace(first=first, hop=hop, across=across, last=last, finish=finish)

    def gram_half(i, h):
        return ((i < 2 * EARLY, gb.at[i, 4 + 6 * h:10 + 6 * h]), (i >= 2 * EARLY, gb.at[i, 10 * h:10 * h + 10]))

    vectors = ring(lambda i, h: ((None, gath.at[i, rows_of[h]]),), fs, fr)
    grams = ring(gram_half, gs, gr)

    halo(0, 0, True)
    halo(0, 1, True)
    for s in range(4):
        acc = halves(mm(stacked(field(s)[...]), wt[:, HALO:HALO + W], True))
        for h in range(2):
            rows = rows_of[h]
            halo(s, h, False)
            wl = halves(mm(stacked(hl[s, rows]), wt[:HALO, :HALO], True))
            wr = halves(mm(stacked(hr[s, rows]), wt[BS:, HALO + W:], True))
            mid = acc[rows]
            parts = [mid[:, :BS] + wl[:, :BS], mid[:, BS:HALO] + wl[:, BS:] + wr[:, :2 * BS], mid[:, HALO:] + wr[:, 2 * BS:]]
            new = jnp.concatenate(parts, axis=1)
            if s:
                new = 2.0 * new - field(s - 1)[rows]
            if s < 3:
                ys[s, rows] = new
                halo(s + 1, h, True)
            else:
                gath[v, rows] = new
                vectors.first(h)

    own = split(gath[v])

    def gram_part(d):
        at = lax.rem(y + NY - d, NY)
        pair = split(gath[pl.ds(at * 2, 2)].reshape(BS, W))
        g = mm3(own, pair, True)
        for t in range(4):
            q = d * 4 + t
            part[q] = g[t * 16:(t + 1) * 16]
            to = device_of(q)
            rel = lax.rem(r - to + NR, NR)

            @pl.when(r != to)
            def _():
                rcopy(part.at[q], inbox.at[rel], ds.at[q], dr.at[rel], (to, v)).start()

    z = r % 8
    zq = (z * 5 + 4) // 8
    mine = (r // 8) * 5 + zq
    active = (zq * 8) // 5 == z

    def share(d):
        @pl.when(active & (mine // 4 == d))
        def _():
            def add(rel, total):
                rcopy(part.at[0], inbox.at[rel], ds.at[0], dr.at[rel], (right, v)).wait_recv()
                return total + inbox[rel]
            gb[v, mine] = lax.fori_loop(1, NR, add, part[mine])

            def send(rel, _):
                rcopy(gb.at[v, mine], gb.at[v, mine], es.at[rel], er.at[mine], (lax.rem(r + rel, NR), v)).start()
                return 0
            lax.fori_loop(1, NR, send, 0)

    def shared(d):
        for q in range(4 * d, 4 * d + 4):
            @pl.when(r != device_of(q))
            def _():
                rcopy(gb.at[v, q], gb.at[v, q], es.at[0], er.at[q], (right, v)).wait_recv()

    vectors.hop(1)
    vectors.across(0)
    gram_part(0)
    vectors.hop(2)
    vectors.across(-1)
    gram_part(1)
    vectors.hop(3)
    vectors.across(-2)
    gram_part(2)
    share(0)
    vectors.across(-3)
    gram_part(3)
    share(1)
    vectors.last()
    vectors.across(4)
    gram_part(4)

    ub = (ub0, ub1, ub2)

    def early(i, core):
        return gb.at[v, :4 * i + 4], ub[i].at[core]

    def send_early(i):
        src, dst = early(i, c)

        @pl.when(y == i)
        def _():
            dst[...] = src[...]
            rcopy(src, dst, us.at[8 * i], ub_sem.at[i], (r, sib)).start()

            def one(m, _):
                rcopy(src, dst, us.at[8 * i + m], ur.at[i], (r, lax.rem(y + m, NY) * 2 + c)).start()
                return 0
            lax.fori_loop(1, NY, one, 0)

    def pass_early(i):
        dst = early(i, c)[1]

        @pl.when(y != i)
        def _():
            rcopy(dst, dst, us.at[0], ur.at[i], (r, sib)).wait_recv()
            rcopy(dst, dst, uf.at[i], ub_sem.at[i], (r, sib)).start()

    def take_early(i):
        dst = early(i, 1 - c)[1]
        rcopy(dst, dst, us.at[0], ub_sem.at[i], (r, sib)).wait_recv()

    shared(0)
    send_early(0)
    shared(1)
    send_early(1)
    for d in range(2, ND):
        share(d)
    shared(2)
    send_early(2)
    grams.first(0)
    pass_early(0)
    pass_early(1)
    shared(3)
    shared(4)
    grams.first(1)
    take_early(0)
    take_early(1)

    def ahead(i, j):
        return ub[i][:, 4 * (i - j):4 * (i - j) + 4].reshape(BS, BS)

    def block(i, j):
        d = i - j
        if d <= 4:
            return gb[2 * i:2 * i + 2, 4 * d:4 * d + 4].reshape(BS, BS)
        d = NB - d
        return gb[2 * j:2 * j + 2, 4 * d:4 * d + 4].reshape(BS, BS).T

    def column(k, first=0):
        top = (k + first) * BS
        s = jnp.concatenate([block(i, k) for i in range(k + first, NB)], axis=0)
        if k:
            rows = (lhi[top:, :k * BS], llo[top:, :k * BS])
            own = (lhi[k * BS:(k + 1) * BS, :k * BS], llo[k * BS:(k + 1) * BS, :k * BS])
            s = s - mm3(rows, own, True)
        return s

    def panel(k, first, rows):
        h, l = split(mm3(split(rows), (whi[k], wlo[k]), True))
        stop = first * BS + rows.shape[0]
        lhi[first * BS:stop, k * BS:(k + 1) * BS] = h
        llo[first * BS:stop, k * BS:(k + 1) * BS] = l
        return h, l

    def after(k):
        whi[k], wlo[k] = split(w_ref[...] * srow[0:1, :])
        if k == 0:
            grams.hop(1)
            low = panel(0, 1, ahead(1, 0))
            a_ref[:BS, :] = ahead(1, 1) - mm3(low, low, True)
            pass_early(2)
        elif k == 1:
            take_early(2)
            grams.hop(2)
            low = panel(0, 2, ahead(2, 0))
            above = (lhi[BS:2 * BS, :BS], llo[BS:2 * BS, :BS])
            next_low = panel(1, 2, ahead(2, 1) - mm3(low, above, True))
            a_ref[:BS, :] = ahead(2, 2) - mm3(low, low, True) - mm3(next_low, next_low, True)
        elif k == 2:
            grams.hop(3)
            for d in (0, -1, -2, -3, 1, 2, 3):
                grams.across(d)
            grams.last()
            grams.across(4)
            for j in range(EARLY):
                panel(j, EARLY, column(j, EARLY - j))
            a_ref[0:M - EARLY * BS, :] = column(EARLY)
        elif k + 1 < NB:
            panel(k, k + 1, a_ref[BS:M - k * BS, :])
            a_ref[0:M - (k + 1) * BS, :] = column(k + 1)

    def step(k, _):
        diag_factor(a_ref, w_ref, srow)
        for kk in range(NB):
            @pl.when(k == kk)
            def _():
                after(kk)
        return 0
    a_ref[:BS, :] = ahead(0, 0)
    lax.fori_loop(0, NB, step, 0)

    sel = lax.broadcasted_iota(jnp.int32, (64, M), 0) + v * 64 == lax.broadcasted_iota(jnp.int32, (64, M), 1)
    r_ref[...] = jnp.where(sel, f32(n_root), 0.0)
    for k in range(NB - 1, -1, -1):
        x = split(mm3(split(r_ref[:, k * BS:(k + 1) * BS]), (whi[k], wlo[k])))
        if k:
            r_ref[:, :k * BS] -= mm3(x, (lhi[k * BS:(k + 1) * BS, :k * BS], llo[k * BS:(k + 1) * BS, :k * BS]))
        xhi[:, k * BS:(k + 1) * BS] = x[0]
        xlo[:, k * BS:(k + 1) * BS] = x[1]
    for d in (1, 2, 3):
        vectors.across(d)
    o_ref[...] = mm3((xhi[...], xlo[...]), split(gath[...].reshape(M, W)))

    for k in waits:
        k.wait_send()
    vectors.finish()
    grams.finish()
    for q in range(NQ):
        @pl.when(r != device_of(q))
        def _():
            rcopy(part.at[q], inbox.at[0], ds.at[q], dr.at[0], (right, v)).wait_send()

    @pl.when(active)
    def _():
        def done(rel, _):
            rcopy(gb.at[v, mine], gb.at[v, mine], es.at[rel], er.at[mine], (right, v)).wait_send()
            return 0
        lax.fori_loop(1, NR, done, 0)

    for i in range(EARLY):
        src, dst = early(i, c)

        @pl.when(y == i)
        def _():
            def sent(m, _):
                rcopy(src, dst, us.at[8 * i + m], ur.at[i], (r, sib)).wait_send()
                return 0
            lax.fori_loop(0, NY, sent, 0)

        @pl.when(y != i)
        def _():
            rcopy(dst, dst, uf.at[i], ub_sem.at[i], (r, sib)).wait_send()


def solve(tiles, columns, start, n_root=128.0):
    vm = pl.BlockSpec(memory_space=pltpu.VMEM)
    dma = pltpu.SemaphoreType.DMA
    return pl.pallas_call(
        functools.partial(kernel, n_root),
        out_shape=jax.ShapeDtypeStruct((64, W), f32),
        in_specs=[pl.BlockSpec(memory_space=pltpu.SMEM), pl.BlockSpec(memory_space=pl.ANY), pl.BlockSpec(memory_space=pl.ANY)],
        out_specs=vm,
        scratch_shapes=[
            pltpu.VMEM((4, 6, BS, BS), bf16), pltpu.VMEM((64, W), f32),
            pltpu.VMEM((W, W + 2 * HALO), bf16), pltpu.VMEM((3, 64, W), f32),
            pltpu.VMEM((4, 64, HALO), f32), pltpu.VMEM((4, 64, HALO), f32),
            pltpu.VMEM((16, 64, W), f32), pltpu.VMEM((16, NQ, 16, BS), f32),
            pltpu.VMEM((2, 4, 16, BS), f32), pltpu.VMEM((2, 8, 16, BS), f32), pltpu.VMEM((2, 12, 16, BS), f32),
            pltpu.VMEM((NQ, 16, BS), f32), pltpu.VMEM((NR, 16, BS), f32),
            pltpu.VMEM((M, BS), f32), pltpu.VMEM((BS, BS), f32), pltpu.VMEM((8, BS), f32),
            pltpu.VMEM((NB, BS, BS), bf16), pltpu.VMEM((NB, BS, BS), bf16),
            pltpu.VMEM((M, M), bf16), pltpu.VMEM((M, M), bf16),
            pltpu.VMEM((64, M), f32), pltpu.VMEM((64, M), bf16), pltpu.VMEM((64, M), bf16),
            dma((2,)), dma((16,)), dma((8,)), dma((8,)), dma((32,)), dma((32,)), dma((32,)), dma((32,)),
            dma((NQ,)), dma((NR,)), dma((NR,)), dma((NQ,)),
            dma((24,)), dma((3,)), dma((3,)), dma((3,))],
        compiler_params=pltpu.CompilerParams(collective_id=0, has_side_effects=True, vmem_limit_bytes=56 << 20),
    )(columns, tiles, start)


def solution(mesh):
    placed = (P("rows", None, None, None), P("rows", None), P("vecs", "rows"))
    return jax.shard_map(
        solve, mesh=mesh, in_specs=placed, out_specs=P("vecs", "rows"), check_vma=False
    )
```

```python
import functools
import types

import jax
import jax.numpy as jnp
from jax import lax
from jax.experimental import pallas as pl
from jax.experimental.pallas import tpu as pltpu
from jax.sharding import PartitionSpec as P

f32, bf16 = jnp.float32, jnp.bfloat16
M, BS, NB, GR = 1024, 128, 8, 8
MESH = pl.DeviceIdType.MESH
NR, NY, ND, NQ = 32, 8, 5, 20
HALO, W, HALF = 384, 512, 32


def split(x):
    hi = x.astype(bf16)
    return hi, (x - hi.astype(f32)).astype(bf16)


def mm(a, b, tb):
    dims = (((1,), (1 if tb else 0,)), ((), ()))
    return lax.dot_general(a, b, dims, preferred_element_type=f32)


def mm3(a, b, tb=False):
    return mm(a[0], b[0], tb) + (mm(a[0], b[1], tb) + mm(a[1], b[0], tb))


def recip(x):
    r = pl.reciprocal(x, approx=True)
    return r * (2.0 - x * r)


def diag_factor(a_ref, w_ref, srow_ref):
    full = a_ref[:BS, :]
    eye = lax.broadcasted_iota(jnp.int32, (BS, BS), 0) == lax.broadcasted_iota(jnp.int32, (BS, BS), 1)
    only = jnp.where(eye, full, 0.0)
    srow = lax.rsqrt(jnp.sum(only, axis=0, keepdims=True))
    srow_ref[...] = jnp.broadcast_to(srow, (8, BS))
    a_ref[:BS, :] = full * srow * lax.rsqrt(jnp.sum(only, axis=1, keepdims=True))
    lane = lax.broadcasted_iota(jnp.int32, (8, BS), 1)
    sub = lax.broadcasted_iota(jnp.int32, (8, BS), 0)
    for g in range(BS // GR):
        lo = g * GR
        ing = (lane >= lo) & (lane < lo + GR)
        p = a_ref[lo:lo + 8, :]
        cols = [jnp.broadcast_to(p[:, lo + j:lo + j + 1], (8, BS)) for j in range(GR)]
        x = jnp.where(lane == sub + lo, 1.0, jnp.where(ing, 0.0, p))
        w = x
        for j in range(0, GR, 2):
            cj, ck = cols[j], cols[j + 1]

            def row(v, i):
                return jnp.broadcast_to(v[i:i + 1, :], (8, BS))
            a, b, c = row(cj, j), row(cj, j + 1), row(ck, j + 1)
            det = a * c - b * b
            pair = (sub == j) | (sub == j + 1)
            cjm = jnp.where(sub == j, -1.0, jnp.where(sub == j + 1, 0.0, cj))
            ckm = jnp.where(sub == j + 1, -1.0, jnp.where(sub == j, 0.0, ck))
            r = recip(det)
            x0, x1 = row(x, j), row(x, j + 1)
            y1 = a * x1 - b * x0
            w = jnp.where(sub == j, x0 * lax.rsqrt(a), jnp.where(sub == j + 1, y1 * lax.rsqrt(a * det), w))
            for m in list(range(j + 2, GR)) + [-1]:
                v = x if m < 0 else cols[m]
                v0, v1 = row(v, j), row(v, j + 1)
                y0 = c * v0 - b * v1
                y1 = a * v1 - b * v0
                z = cjm * y0 + ckm * y1
                new = jnp.where(pair, 0.0, v) - r * z
                if m < 0:
                    x = new
                else:
                    cols[m] = new
        w_ref[lo:lo + 8, :] = jnp.where(lane < lo + GR, w, 0.0)
        for h in range(g + 1, BS // GR):
            q = a_ref[h * 8:h * 8 + 8, :]
            cs = [jnp.broadcast_to(q[:, lo + j:lo + j + 1], (8, BS)) for j in range(GR)]
            t = [cs[j] * jnp.broadcast_to(x[j:j + 1, :], (8, BS)) for j in range(GR)]
            while len(t) > 1:
                t = [t[i] + t[i + 1] for i in range(0, len(t), 2)]
            a_ref[h * 8:h * 8 + 8, :] = jnp.where(ing, 0.0, q) - t[0]


def device_of(q):
    return (q * 8) // 5


EARLY = 3


def kernel(n_root, columns_ref, tiles_in, y0_in, o_ref, tiles_ref, y0_ref, wt, ys, hl, hr, gath, gb, ub0, ub1, ub2, part, inbox,
           a_ref, w_ref, srow, whi, wlo, lhi, llo, r_ref, xhi, xlo,
           ls, hs, hrl, hrr, fs, fr, gs, gr, ds, dr, es, er, us, ur, uf, ub_sem):
    loads = [pltpu.make_async_copy(a, b, ls.at[n]) for n, (a, b) in enumerate(((y0_in, y0_ref), (tiles_in, tiles_ref)))]
    for load in loads:
        load.start()
    r, v = lax.axis_index("rows"), lax.axis_index("vecs")
    y, c = v // 2, v % 2
    sib, yr, yl = y * 2 + 1 - c, lax.rem(y + 1, NY) * 2 + c, lax.rem(y + NY - 1, NY) * 2 + c
    right, left = lax.rem(r + 1, NR), lax.rem(r + NR - 1, NR)

    barrier = pltpu.get_barrier_semaphore()

    def greet(d, _):
        pl.semaphore_signal(barrier, inc=1, device_id=(lax.rem(r + d, NR), v), device_id_type=MESH)
        return 0
    lax.fori_loop(1, NR, greet, 0)

    def greet_y(d, _):
        pl.semaphore_signal(barrier, inc=1, device_id=(r, lax.rem(y + d, NY) * 2 + c), device_id_type=MESH)
        return 0
    lax.fori_loop(1, NY, greet_y, 0)
    pl.semaphore_signal(barrier, inc=1, device_id=(r, sib), device_id_type=MESH)

    def rcopy(src, dst, send, recv, to):
        return pltpu.make_async_remote_copy(src_ref=src, dst_ref=dst, send_sem=send, recv_sem=recv, device_id=to, device_id_type=MESH)

    for load in loads:
        load.wait()
    wt[...] = jnp.zeros_like(wt)
    for b in range(4):
        rows = slice(b * BS, (b + 1) * BS)
        for t, o in ((0, 0), (1, -1), (2, 1)):
            wt[rows, (b + 3 + o) * BS:(b + 4 + o) * BS] = tiles_ref[b, t]
        for o in (-3, -2, 2, 3):
            want = lax.rem(r * 4 + b + o + 4 * NR, 4 * NR)
            tile = jnp.zeros((BS, BS), bf16)
            for t in (3, 4, 5):
                tile = jnp.where(columns_ref[b, t] == want, tiles_ref[b, t], tile)
            wt[rows, (b + 3 + o) * BS:(b + 4 + o) * BS] = tile

    pl.semaphore_wait(barrier, NR - 1 + NY - 1 + 1)

    def stacked(x):
        return jnp.concatenate(split(x), axis=0)

    def halves(x):
        n = x.shape[0] // 2
        return x[:n] + x[n:]

    waits = []
    rows_of = (slice(0, HALF), slice(HALF, 2 * HALF))

    def field(s):
        return y0_ref if s == 0 else ys.at[s - 1]

    def halo(s, h, go):
        src, n = field(s), 2 * s + h
        to_right = rcopy(src.at[:, W - HALO:], hl.at[s], hs.at[2 * n], hrl.at[n], (right, v))
        to_left = rcopy(src.at[:, :HALO], hr.at[s], hs.at[2 * n + 1], hrr.at[n], (left, v))
        if go:
            to_right.start()
            to_left.start()
            waits.extend((to_right, to_left))
        else:
            to_right.wait_recv()
            to_left.wait_recv()

    def ring(half, send, recv):
        started = set()

        def slot(d):
            return lax.rem(y + NY + d, NY) * 2 + c

        def other(d):
            return lax.rem(y + NY + d, NY) * 2 + 1 - c

        def each(i, h, act):
            for when, ref in half(i, h):
                if when is None:
                    act(ref)
                else:
                    @pl.when(when)
                    def _():
                        act(ref)

        def go(i, n, h, to):
            each(i, h, lambda ref: rcopy(ref, ref, send.at[2 * n + h], recv.at[2 * n + h], (r, to)).start())
            started.add((n, h))

        def arrive(i, n, h):
            each(i, h, lambda ref: rcopy(ref, ref, send.at[2 * n + h], recv.at[2 * n + h], (r, sib)).wait_recv())

        def origin(n):
            if n < 4:
                return slot(-n)
            if n < 8:
                return slot(n - 4)
            return slot(n - 11) if n < 15 else slot(4)

        def finish():
            for n, h in sorted(started):
                each(origin(n), h, lambda ref: rcopy(ref, ref, send.at[2 * n + h], recv.at[2 * n + h], (r, sib)).wait_send())

        def first(h):
            go(v, 0, h, yr)
            go(v, 4, h, yl)
            go(v, 11, h, sib)

        def hop(s):
            for h in range(2):
                arrive(slot(-s), s - 1, h)
                if s < 3 or h == 0:
                    go(slot(-s), s, h, yr)
                go(slot(-s), 11 - s, h, sib)
                arrive(slot(s), 3 + s, h)
                if s < 3 or h == 1:
                    go(slot(s), 4 + s, h, yl)
                go(slot(s), 11 + s, h, sib)

        def across(d):
            for h in range(2):
                arrive(other(d), 15 if d == 4 else 11 + d, h)

        def last():
            arrive(slot(4), 3, 0)
            go(slot(4), 15, 0, sib)
            arrive(slot(4), 7, 1)
            go(slot(4), 15, 1, sib)
        return types.SimpleNamespace(first=first, hop=hop, across=across, last=last, finish=finish)

    def gram_half(i, h):
        return ((i < 2 * EARLY, gb.at[i, 4 + 6 * h:10 + 6 * h]), (i >= 2 * EARLY, gb.at[i, 10 * h:10 * h + 10]))

    vectors = ring(lambda i, h: ((None, gath.at[i, rows_of[h]]),), fs, fr)
    grams = ring(gram_half, gs, gr)

    halo(0, 0, True)
    for s in range(4):
        acc = halves(mm(stacked(field(s)[...]), wt[:, HALO:HALO + W], True))
        for h in range(1):
            rows = slice(0, 64)
            halo(s, h, False)
            wl = halves(mm(stacked(hl[s, rows]), wt[:HALO, :HALO], True))
            wr = halves(mm(stacked(hr[s, rows]), wt[BS:, HALO + W:], True))
            mid = acc[rows]
            parts = [mid[:, :BS] + wl[:, :BS], mid[:, BS:HALO] + wl[:, BS:] + wr[:, :2 * BS], mid[:, HALO:] + wr[:, 2 * BS:]]
            new = jnp.concatenate(parts, axis=1)
            if s:
                new = 2.0 * new - field(s - 1)[rows]
            if s < 3:
                ys[s, rows] = new
                halo(s + 1, h, True)
            else:
                gath[v, rows] = new
                vectors.first(0)
                vectors.first(1)

    own = split(gath[v])

    def gram_part(d):
        at = lax.rem(y + NY - d, NY)
        pair = split(gath[pl.ds(at * 2, 2)].reshape(BS, W))
        g = mm3(own, pair, True)
        for t in range(4):
            q = d * 4 + t
            part[q] = g[t * 16:(t + 1) * 16]
            to = device_of(q)
            rel = lax.rem(r - to + NR, NR)

            @pl.when(r != to)
            def _():
                rcopy(part.at[q], inbox.at[rel], ds.at[q], dr.at[rel], (to, v)).start()

    z = r % 8
    zq = (z * 5 + 4) // 8
    mine = (r // 8) * 5 + zq
    active = (zq * 8) // 5 == z

    def share(d):
        @pl.when(active & (mine // 4 == d))
        def _():
            def add(rel, total):
                rcopy(part.at[0], inbox.at[rel], ds.at[0], dr.at[rel], (right, v)).wait_recv()
                return total + inbox[rel]
            gb[v, mine] = lax.fori_loop(1, NR, add, part[mine])

            def send(rel, _):
                rcopy(gb.at[v, mine], gb.at[v, mine], es.at[rel], er.at[mine], (lax.rem(r + rel, NR), v)).start()
                return 0
            lax.fori_loop(1, NR, send, 0)

    def shared(d):
        for q in range(4 * d, 4 * d + 4):
            @pl.when(r != device_of(q))
            def _():
                rcopy(gb.at[v, q], gb.at[v, q], es.at[0], er.at[q], (right, v)).wait_recv()

    vectors.hop(1)
    vectors.across(0)
    gram_part(0)
    vectors.hop(2)
    vectors.across(-1)
    gram_part(1)
    vectors.hop(3)
    vectors.across(-2)
    gram_part(2)
    share(0)
    vectors.across(-3)
    gram_part(3)
    share(1)
    vectors.last()
    vectors.across(4)
    gram_part(4)

    ub = (ub0, ub1, ub2)

    def early(i, core):
        return gb.at[v, :4 * i + 4], ub[i].at[core]

    def send_early(i):
        src, dst = early(i, c)

        @pl.when(y == i)
        def _():
            dst[...] = src[...]
            rcopy(src, dst, us.at[8 * i], ub_sem.at[i], (r, sib)).start()

            def one(m, _):
                rcopy(src, dst, us.at[8 * i + m], ur.at[i], (r, lax.rem(y + m, NY) * 2 + c)).start()
                return 0
            lax.fori_loop(1, NY, one, 0)

    def pass_early(i):
        dst = early(i, c)[1]

        @pl.when(y != i)
        def _():
            rcopy(dst, dst, us.at[0], ur.at[i], (r, sib)).wait_recv()
            rcopy(dst, dst, uf.at[i], ub_sem.at[i], (r, sib)).start()

    def take_early(i):
        dst = early(i, 1 - c)[1]
        rcopy(dst, dst, us.at[0], ub_sem.at[i], (r, sib)).wait_recv()

    shared(0)
    send_early(0)
    shared(1)
    send_early(1)
    for d in range(2, ND):
        share(d)
    shared(2)
    send_early(2)
    grams.first(0)
    pass_early(0)
    pass_early(1)
    shared(3)
    shared(4)
    grams.first(1)
    take_early(0)
    take_early(1)

    def ahead(i, j):
        return ub[i][:, 4 * (i - j):4 * (i - j) + 4].reshape(BS, BS)

    def block(i, j):
        d = i - j
        if d <= 4:
            return gb[2 * i:2 * i + 2, 4 * d:4 * d + 4].reshape(BS, BS)
        d = NB - d
        return gb[2 * j:2 * j + 2, 4 * d:4 * d + 4].reshape(BS, BS).T

    def column(k, first=0):
        top = (k + first) * BS
        s = jnp.concatenate([block(i, k) for i in range(k + first, NB)], axis=0)
        if k:
            rows = (lhi[top:, :k * BS], llo[top:, :k * BS])
            own = (lhi[k * BS:(k + 1) * BS, :k * BS], llo[k * BS:(k + 1) * BS, :k * BS])
            s = s - mm3(rows, own, True)
        return s

    def panel(k, first, rows):
        h, l = split(mm3(split(rows), (whi[k], wlo[k]), True))
        stop = first * BS + rows.shape[0]
        lhi[first * BS:stop, k * BS:(k + 1) * BS] = h
        llo[first * BS:stop, k * BS:(k + 1) * BS] = l
        return h, l

    def after(k):
        whi[k], wlo[k] = split(w_ref[...] * srow[0:1, :])
        if k == 0:
            grams.hop(1)
            low = panel(0, 1, ahead(1, 0))
            a_ref[:BS, :] = ahead(1, 1) - mm3(low, low, True)
            pass_early(2)
        elif k == 1:
            take_early(2)
            grams.hop(2)
            low = panel(0, 2, ahead(2, 0))
            above = (lhi[BS:2 * BS, :BS], llo[BS:2 * BS, :BS])
            next_low = panel(1, 2, ahead(2, 1) - mm3(low, above, True))
            a_ref[:BS, :] = ahead(2, 2) - mm3(low, low, True) - mm3(next_low, next_low, True)
        elif k == 2:
            grams.hop(3)
            for d in (0, -1, -2, -3, 1, 2, 3):
                grams.across(d)
            grams.last()
            grams.across(4)
            for j in range(EARLY):
                panel(j, EARLY, column(j, EARLY - j))
            a_ref[0:M - EARLY * BS, :] = column(EARLY)
        elif k + 1 < NB:
            panel(k, k + 1, a_ref[BS:M - k * BS, :])
            a_ref[0:M - (k + 1) * BS, :] = column(k + 1)

    def step(k, _):
        diag_factor(a_ref, w_ref, srow)
        for kk in range(NB):
            @pl.when(k == kk)
            def _():
                after(kk)
        return 0
    a_ref[:BS, :] = ahead(0, 0)
    lax.fori_loop(0, NB, step, 0)

    sel = lax.broadcasted_iota(jnp.int32, (64, M), 0) + v * 64 == lax.broadcasted_iota(jnp.int32, (64, M), 1)
    r_ref[...] = jnp.where(sel, f32(n_root), 0.0)
    for k in range(NB - 1, -1, -1):
        x = split(mm3(split(r_ref[:, k * BS:(k + 1) * BS]), (whi[k], wlo[k])))
        if k:
            r_ref[:, :k * BS] -= mm3(x, (lhi[k * BS:(k + 1) * BS, :k * BS], llo[k * BS:(k + 1) * BS, :k * BS]))
        xhi[:, k * BS:(k + 1) * BS] = x[0]
        xlo[:, k * BS:(k + 1) * BS] = x[1]
    for d in (1, 2, 3):
        vectors.across(d)
    o_ref[...] = mm3((xhi[...], xlo[...]), split(gath[...].reshape(M, W)))

    for k in waits:
        k.wait_send()
    vectors.finish()
    grams.finish()
    for q in range(NQ):
        @pl.when(r != device_of(q))
        def _():
            rcopy(part.at[q], inbox.at[0], ds.at[q], dr.at[0], (right, v)).wait_send()

    @pl.when(active)
    def _():
        def done(rel, _):
            rcopy(gb.at[v, mine], gb.at[v, mine], es.at[rel], er.at[mine], (right, v)).wait_send()
            return 0
        lax.fori_loop(1, NR, done, 0)

    for i in range(EARLY):
        src, dst = early(i, c)

        @pl.when(y == i)
        def _():
            def sent(m, _):
                rcopy(src, dst, us.at[8 * i + m], ur.at[i], (r, sib)).wait_send()
                return 0
            lax.fori_loop(0, NY, sent, 0)

        @pl.when(y != i)
        def _():
            rcopy(dst, dst, uf.at[i], ub_sem.at[i], (r, sib)).wait_send()


def solve(tiles, columns, start, n_root=128.0):
    vm = pl.BlockSpec(memory_space=pltpu.VMEM)
    dma = pltpu.SemaphoreType.DMA
    return pl.pallas_call(
        functools.partial(kernel, n_root),
        out_shape=jax.ShapeDtypeStruct((64, W), f32),
        in_specs=[pl.BlockSpec(memory_space=pltpu.SMEM), pl.BlockSpec(memory_space=pl.ANY), pl.BlockSpec(memory_space=pl.ANY)],
        out_specs=vm,
        scratch_shapes=[
            pltpu.VMEM((4, 6, BS, BS), bf16), pltpu.VMEM((64, W), f32),
            pltpu.VMEM((W, W + 2 * HALO), bf16), pltpu.VMEM((3, 64, W), f32),
            pltpu.VMEM((4, 64, HALO), f32), pltpu.VMEM((4, 64, HALO), f32),
            pltpu.VMEM((16, 64, W), f32), pltpu.VMEM((16, NQ, 16, BS), f32),
            pltpu.VMEM((2, 4, 16, BS), f32), pltpu.VMEM((2, 8, 16, BS), f32), pltpu.VMEM((2, 12, 16, BS), f32),
            pltpu.VMEM((NQ, 16, BS), f32), pltpu.VMEM((NR, 16, BS), f32),
            pltpu.VMEM((M, BS), f32), pltpu.VMEM((BS, BS), f32), pltpu.VMEM((8, BS), f32),
            pltpu.VMEM((NB, BS, BS), bf16), pltpu.VMEM((NB, BS, BS), bf16),
            pltpu.VMEM((M, M), bf16), pltpu.VMEM((M, M), bf16),
            pltpu.VMEM((64, M), f32), pltpu.VMEM((64, M), bf16), pltpu.VMEM((64, M), bf16),
            dma((2,)), dma((16,)), dma((8,)), dma((8,)), dma((32,)), dma((32,)), dma((32,)), dma((32,)),
            dma((NQ,)), dma((NR,)), dma((NR,)), dma((NQ,)),
            dma((24,)), dma((3,)), dma((3,)), dma((3,))],
        compiler_params=pltpu.CompilerParams(collective_id=0, has_side_effects=True, vmem_limit_bytes=56 << 20),
    )(columns, tiles, start)


def solution(mesh):
    placed = (P("rows", None, None, None), P("rows", None), P("vecs", "rows"))
    return jax.shard_map(
        solve, mesh=mesh, in_specs=placed, out_specs=P("vecs", "rows"), check_vma=False
    )
```
